128 devices in a mesh: dp: 4 (over x), head: 2 (over z_hi), ctx: 16 (over z_lo, y, core).
Axes of the slice: x: 4, y: 4, z: 4 (z_hi: 2, z_lo: 2; z = z_hi * 2 + z_lo), core: 2. Of those that a mesh axis runs over, the one named last changes fastest.
Arguments:
- query_input: bfloat16 [4, 3072, 2560], P('dp', 'ctx', 'head'), may hold values from -2700 to 2700
- key_input: bfloat16 [4, 3072, 2560], P('dp', 'ctx', 'head'), may hold values from -2700 to 2700
- value_input: bfloat16 [4, 3072, 2560], P('dp', 'ctx', 'head'), may hold values from -6 to 6
- query_tangent: bfloat16 [4, 3072, 2560], P('dp', 'ctx', 'head'), may hold values from -2700 to 2700
- key_tangent: bfloat16 [4, 3072, 2560], P('dp', 'ctx', 'head'), may hold values from -2700 to 2700
- value_tangent: bfloat16 [4, 3072, 2560], P('dp', 'ctx', 'head'), may hold values from -6 to 6
- query_gain: float32 [2560], P('head'), may hold values from 0.8 to 2
- key_gain: float32 [2560], P('head'), may hold values from 0.8 to 2
- out_weight: bfloat16 [2560, 5120], P('head', 'dp'), may hold values from -0.125 to 0.125
- span_order: int32 [32], replicated, may hold values from 0 to 31, each once
Outputs:
- projected: bfloat16 [4, 3072, 5120], P('dp', 'ctx', 'head')
- projected_tangent: bfloat16 [4, 3072, 5120], P('dp', 'ctx', 'head')
The draws below stay inside these ranges and needn't reach their ends.
Inputs may be any that keep to these rules, and one draw needn't show every extreme that they name: `span_order`: each span number appears once.
All inputs are finite; a program needn't handle non-finite values.
Results may differ from the reference program's by a relative error of at most 0.006.
The reference program's roundings to bfloat16 on the way count: a program that leaves them out, or rounds other values in their place, can miss the bound.
Values may be sent and summed in bfloat16 or wider, within the bound.
No kernel may reach another device: no remote copies, remote signals or barrier semaphores. Data moves between devices by JAX's collectives and lax.ppermute only.
A program may use at most 128 MiB of HBM per device.

```python
import math
import jax
import jax.numpy as jnp
from jax import lax

D = 5120
HEADS = 20
HEAD_DIM = 128
GRID_H = 8
GRID_W = 16
CAP = 30
HD = 2560
SPAN = 96
SPANS = 32
SEQ = 3072
CLIPS = 4


def side_scales(base_key, salt, power):
    base_key = jax.random.fold_in(base_key, salt)
    key_rows, key_columns = jax.random.split(base_key)
    row_scale = jnp.exp(jnp.log(10.0) * jax.random.uniform(key_rows, (CLIPS, SEQ, 1)))
    head_place = (jnp.arange(HD) // HEAD_DIM).astype(jnp.float32) / (HEADS - 1)
    column_scale = jnp.exp(jnp.log(10.0) * jax.random.uniform(key_columns, (HD,)) + power * jnp.log(3.0) * head_place)
    return row_scale * column_scale


def mixed_values(base_key):
    key_normal = jax.random.fold_in(base_key, 0)
    full_shape = (CLIPS, SEQ, HD)
    normal_draw = jnp.clip(jax.random.normal(key_normal, full_shape), -6.0, 6.0)
    return normal_draw


def draw_query_input(key, part):
    power = 1.0
    scales = side_scales(key, 7, power)
    key = jax.random.fold_in(key, 1)
    return (mixed_values(key) * scales).astype(jnp.bfloat16)


def draw_query_tangent(key, part):
    power = 1.0
    scales = side_scales(key, 7, power)
    key = jax.random.fold_in(key, 2)
    return (mixed_values(key) * scales).astype(jnp.bfloat16)


def draw_key_input(key, part):
    power = 1.0
    scales = side_scales(key, 8, power)
    key = jax.random.fold_in(key, 3)
    return (mixed_values(key) * scales).astype(jnp.bfloat16)


def draw_key_tangent(key, part):
    power = 1.0
    scales = side_scales(key, 8, power)
    key = jax.random.fold_in(key, 4)
    return (mixed_values(key) * scales).astype(jnp.bfloat16)


def block_scale(rng, shape, shards, smallest, largest):
    level, own = 1.0, jax.random.fold_in(rng, 6)
    for position, parts in shards:
        draws = jnp.exp(jax.random.uniform(jax.random.fold_in(own, position), (parts,), jnp.float32, smallest / len(shards), largest / len(shards)))
        level = level * jnp.repeat(draws, shape[position] // parts).reshape([-1 if axis == position else 1 for axis in range(len(shape))])
    return level


def bell_draw(rng, shape, spread, most, cuts=(), kind=jnp.bfloat16):
    drawn = spread * jax.random.normal(rng, shape, jnp.float32)
    if cuts:
        drawn = drawn * block_scale(rng, shape, cuts, -0.22, 0.18)
    return jnp.clip(drawn, -most, most).astype(kind)


def setup_inputs(seed: int = 0) -> dict:
    streams_of = jax.random.split(jax.random.key(seed), 11)
    return {
        "query_input": draw_query_input(jax.random.fold_in(streams_of[10], 71), 0),
        "key_input": draw_key_input(jax.random.fold_in(streams_of[10], 71), 0),
        "value_input": bell_draw(streams_of[2], (CLIPS, SEQ, HD), 1.0, 6.0, ((0, 4), (1, 16), (2, 2))),
        "query_tangent": draw_query_tangent(jax.random.fold_in(streams_of[10], 71), 0),
        "key_tangent": draw_key_tangent(jax.random.fold_in(streams_of[10], 71), 0),
        "value_tangent": bell_draw(streams_of[5], (CLIPS, SEQ, HD), 1.0, 6.0, ((0, 4), (1, 16), (2, 2))),
        "query_gain": jnp.clip(jnp.exp(math.log(2.0) - 0.9162907 * jax.random.uniform(streams_of[6], (HD,), jnp.float32) ** block_scale(streams_of[6], (HD,), ((0, 2),), -0.2, 0.2)), 0.8, 2.0),
        "key_gain": jnp.clip(jnp.exp(math.log(2.0) - 0.9162907 * jax.random.uniform(streams_of[7], (HD,), jnp.float32) ** block_scale(streams_of[7], (HD,), ((0, 2),), -0.2, 0.2)), 0.8, 2.0),
        "out_weight": bell_draw(streams_of[8], (HD, D), HD ** -0.5, 0.125, ((0, 2), (1, 4))),
        "span_order": jax.random.permutation(streams_of[9], SPANS).astype(jnp.int32),
    }


def rope_angles(positions):
    pair_count = HEAD_DIM // 2
    side_pairs = pair_count // 3
    time_pairs = pair_count - 2 * side_pairs
    frame_index = (positions // (GRID_H * GRID_W)).astype(jnp.float32)
    grid_row = (positions // GRID_W % GRID_H).astype(jnp.float32)
    grid_column = (positions % GRID_W).astype(jnp.float32)
    time_freq = 10000.0 ** (-jnp.arange(time_pairs, dtype=jnp.float32) / time_pairs)
    side_freq = 10000.0 ** (-jnp.arange(side_pairs, dtype=jnp.float32) / side_pairs)
    angle_table = jnp.concatenate([frame_index[:, None] * time_freq[None, :], grid_row[:, None] * side_freq[None, :], grid_column[:, None] * side_freq[None, :]], axis=1)
    angle_table = jnp.repeat(angle_table, 2, axis=1)
    return (jnp.cos(angle_table), jnp.sin(angle_table))

def partner(features):
    parity = jnp.arange(features.shape[-1]) % 2 == 0
    return jnp.where(parity, -jnp.roll(features, -1, axis=-1), jnp.roll(features, 1, axis=-1))

def norm_rope(raw_rows, tangent_rows, square_sum, mixed_sum, gain_row, cosine_table, sine_table):
    inverse = lax.rsqrt(square_sum / HD + 1e-06)[..., None, None]
    mixing = (mixed_sum / HD)[..., None, None]
    head_gain = gain_row.reshape(-1, HEAD_DIM)
    normed = head_gain * raw_rows * inverse
    normed_tangent = head_gain * (tangent_rows * inverse - raw_rows * mixing * inverse * inverse * inverse)
    cosine_wide = cosine_table[:, None, :]
    sine_wide = sine_table[:, None, :]
    turned = normed * cosine_wide + partner(normed) * sine_wide
    turned_tangent = normed_tangent * cosine_wide + partner(normed_tangent) * sine_wide
    return (turned.astype(jnp.bfloat16), turned_tangent.astype(jnp.bfloat16))

def one_head(head_items):
    queries, queries_tangent, key_rows, key_rows_tangent, value_rows, value_rows_tangent = head_items
    score_scale = 1.0 / math.sqrt(HEAD_DIM)
    scores = jnp.dot(queries, key_rows.T, preferred_element_type=jnp.float32) * score_scale
    scores_tangent = (jnp.dot(queries_tangent, key_rows.T, preferred_element_type=jnp.float32) + jnp.dot(queries, key_rows_tangent.T, preferred_element_type=jnp.float32)) * score_scale
    squashed = jnp.tanh(scores / CAP)
    weights = jnp.exp(CAP * squashed)
    weights_tangent = weights * ((1.0 - squashed * squashed) * scores_tangent)
    norm_sum = lax.optimization_barrier(jnp.sum(weights, axis=1))
    tangent_sum = lax.optimization_barrier(jnp.sum(weights_tangent, axis=1))
    weights_low = weights.astype(jnp.bfloat16)
    weights_low_tangent = weights_tangent.astype(jnp.bfloat16)
    weighted = jnp.dot(weights_low, value_rows, preferred_element_type=jnp.float32)
    weighted_tangent = jnp.dot(weights_low, value_rows_tangent, preferred_element_type=jnp.float32) + jnp.dot(weights_low_tangent, value_rows, preferred_element_type=jnp.float32)
    attention = weighted / norm_sum[:, None]
    attention_tangent = weighted_tangent / norm_sum[:, None] - (tangent_sum / norm_sum)[:, None] * attention
    return (attention.astype(jnp.bfloat16), attention_tangent.astype(jnp.bfloat16))

def heads_first(tensor):
    return tensor.reshape(CLIPS, SEQ, HEADS, HEAD_DIM).transpose(0, 2, 1, 3).reshape(CLIPS * HEADS, SEQ, HEAD_DIM)

def features_last(tensor):
    return tensor.reshape(CLIPS, HEADS, SEQ, HEAD_DIM).transpose(0, 2, 1, 3).reshape(CLIPS * SEQ, HD)

def reference(query_input, key_input, value_input, query_tangent, key_tangent, value_tangent, query_gain, key_gain, out_weight, span_order):
    positions = (span_order[:, None] * SPAN + jnp.arange(SPAN, dtype=jnp.int32)[None, :]).reshape(-1)
    cosine_table, sine_table = rope_angles(positions)
    head_shape = (CLIPS, SEQ, HEADS, HEAD_DIM)

    def prepare(raw_rows, tangent_rows, gain_row):
        raw_float = raw_rows.astype(jnp.float32)
        tangent_float = tangent_rows.astype(jnp.float32)
        square_sum = lax.optimization_barrier(jnp.sum(raw_float * raw_float, axis=-1))
        mixed_sum = lax.optimization_barrier(jnp.sum(raw_float * tangent_float, axis=-1))
        return norm_rope(raw_float.reshape(head_shape), tangent_float.reshape(head_shape), square_sum, mixed_sum, gain_row, cosine_table, sine_table)
    query_turned, query_turned_tangent = prepare(query_input, query_tangent, query_gain)
    key_turned, key_turned_tangent = prepare(key_input, key_tangent, key_gain)
    head_items = (heads_first(query_turned), heads_first(query_turned_tangent), heads_first(key_turned), heads_first(key_turned_tangent), heads_first(value_input), heads_first(value_tangent))
    attention, attention_tangent = lax.map(one_head, head_items)
    projected = jnp.dot(features_last(attention), out_weight, preferred_element_type=jnp.float32).astype(jnp.bfloat16).reshape(CLIPS, SEQ, D)
    projected_tangent = jnp.dot(features_last(attention_tangent), out_weight, preferred_element_type=jnp.float32).astype(jnp.bfloat16).reshape(CLIPS, SEQ, D)
    return (projected, projected_tangent)
```

```python
import functools
import math

import jax
import jax.numpy as jnp
from jax import lax
from jax.experimental import pallas as pl
from jax.experimental.pallas import tpu as pltpu
from jax.sharding import PartitionSpec as P

HEAD_DIM = 128
GRID_H = 8
GRID_W = 16
CAP = 30
HD = 2560
SPAN = 96
ROWS = 192
HEADS = 10
FEATURES = HEADS * HEAD_DIM
CHIPS = 8
PART = 48
SLOT = ROWS + PART
TILE_Q = 384
TILE_K = 512
SCALE = 1.0 / math.sqrt(HEAD_DIM)
BF16 = jnp.bfloat16
F32 = jnp.float32
MIB = 2**20
SMEM = pl.BlockSpec(memory_space=pltpu.SMEM)


def params(mib):
    return pltpu.CompilerParams(vmem_limit_bytes=mib * MIB)


def cost(flops, moved):
    return pl.CostEstimate(flops=flops, bytes_accessed=moved, transcendentals=0)


def shape(*dims, kind=BF16):
    return jax.ShapeDtypeStruct(dims, kind)


def whole(member):
    return pl.BlockSpec(member.shape, lambda step: (0,) * len(member.shape))


def call(kernel, name, outs, operands, scratch, mib, estimate, scalars=0):
    return pl.pallas_call(
        kernel,
        grid=(1,),
        out_shape=outs,
        in_specs=[SMEM] * scalars + [whole(member) for member in operands[scalars:]],
        out_specs=jax.tree.map(whole, outs),
        scratch_shapes=scratch,
        compiler_params=params(mib),
        cost_estimate=estimate,
        name=name,
    )(*operands)


def dot(left, right):
    return lax.dot_general(left, right, (((1,), (0,)), ((), ())), preferred_element_type=F32)


def dot_rows(left, right):
    return lax.dot_general(left, right, (((1,), (1,)), ((), ())), preferred_element_type=F32)


def head_columns(head):
    return pl.ds(pl.multiple_of(head * HEAD_DIM, HEAD_DIM), HEAD_DIM)


def rope_tables(own_spans):
    positions = (
        own_spans[:, None] * SPAN + jnp.arange(SPAN, dtype=jnp.int32)[None, :]
    ).reshape(-1)
    pairs = HEAD_DIM // 2
    side = pairs // 3
    time = pairs - 2 * side
    time_freq = 10000.0 ** (-jnp.arange(time, dtype=F32) / time)
    side_freq = 10000.0 ** (-jnp.arange(side, dtype=F32) / side)
    freq = jnp.concatenate([time_freq, side_freq, side_freq])
    freq = jnp.broadcast_to(freq[:, None], (pairs, 2)).reshape(1, HEAD_DIM)
    pair = (jnp.arange(HEAD_DIM, dtype=jnp.int32) // 2)[None, :]
    place = jnp.where(
        pair < time,
        (positions // (GRID_H * GRID_W))[:, None],
        jnp.where(
            pair < time + side,
            (positions // GRID_W % GRID_H)[:, None],
            (positions % GRID_W)[:, None],
        ),
    ).astype(F32)
    angle = place * freq
    return jnp.cos(angle), jnp.sin(angle)


def prepare_kernel(meta, q, qt, k, kt, v, vt, *outs):
    stats = outs[CHIPS]
    chip = meta[0]
    for slot in range(CHIPS):
        other = jnp.bitwise_xor(chip, slot)
        for place, head in ((0, other), (1, CHIPS + other // 4)):
            outs[slot][place, :, :HEAD_DIM] = v[:, head_columns(head)]
            outs[slot][place, :, HEAD_DIM:] = vt[:, head_columns(head)]
    lane = lax.broadcasted_iota(jnp.int32, (ROWS, HEAD_DIM), 1)
    total = jnp.zeros((ROWS, HEAD_DIM), F32)
    for place, (left, right) in enumerate(((q, q), (q, qt), (k, k), (k, kt))):
        product = left[...].astype(F32) * right[...].astype(F32)
        total = jnp.where(lane == place, jnp.sum(product, axis=1, keepdims=True), total)
    stats[...] = total


def prepare(meta, q, qt, k, kt, v, vt):
    return call(
        prepare_kernel,
        "prepare",
        [shape(2, ROWS, 256)] * CHIPS + [shape(ROWS, HEAD_DIM, kind=F32)],
        [meta, q, qt, k, kt, v, vt],
        [],
        60,
        cost(4 * ROWS * FEATURES, 6 * MIB),
        1,
    )


def norm_rope_kernel(meta, q, qt, k, kt, mine, theirs, q_gain, k_gain, cosine, sine, *rest):
    q_out, k_out = rest[:CHIPS], rest[CHIPS : 2 * CHIPS]
    q_extra, k_extra = rest[2 * CHIPS :]
    chip = meta[0]
    stats = mine[...] + theirs[...]
    cos = cosine[...]
    even = lax.broadcasted_iota(jnp.int32, (ROWS, HEAD_DIM), 1) % 2 == 0
    sin_next = jnp.where(even, -sine[...], 0.0)
    sin_last = jnp.where(even, 0.0, sine[...])

    def rotated(x):
        after = pltpu.roll(x, HEAD_DIM - 1, 1)
        before = pltpu.roll(x, 1, 1)
        return (x * cos + (after * sin_next + before * sin_last)).astype(BF16)

    def of_head(raw_ref, tangent_ref, gain_ref, inverse, mixing, head):
        columns = head_columns(head)
        raw = raw_ref[:, columns].astype(F32)
        tangent = tangent_ref[:, columns].astype(F32)
        gain = gain_ref[:, columns]
        normed = gain * raw * inverse
        normed_tangent = gain * (
            tangent * inverse - raw * mixing * inverse * inverse * inverse
        )
        return rotated(normed), rotated(normed_tangent)

    wide = (ROWS, HEAD_DIM)
    for first, raw_ref, tangent_ref, gain_ref, outs, extra in (
        (0, q, qt, q_gain, q_out, q_extra),
        (2, k, kt, k_gain, k_out, k_extra),
    ):
        inverse = jnp.broadcast_to(lax.rsqrt(stats[:, first : first + 1] / HD + 1e-06), wide)
        mixing = jnp.broadcast_to(stats[:, first + 1 : first + 2] / HD, wide)
        for shared in range(2):
            turned, turned_tangent = of_head(
                raw_ref, tangent_ref, gain_ref, inverse, mixing, CHIPS + shared
            )
            extra[shared, :, :HEAD_DIM] = turned
            extra[shared, :, HEAD_DIM:] = turned_tangent
        for slot in range(CHIPS):
            other = jnp.bitwise_xor(chip, slot)
            turned, turned_tangent = of_head(
                raw_ref, tangent_ref, gain_ref, inverse, mixing, other
            )
            if first == 0:
                outs[slot][:ROWS, :HEAD_DIM] = turned
                outs[slot][:ROWS, HEAD_DIM:] = turned_tangent
                start = pl.multiple_of(other % 4 * PART, 16)
                outs[slot][ROWS:] = extra[other // 4, pl.ds(start, PART)]
            else:
                outs[slot][0, :, :HEAD_DIM] = turned
                outs[slot][0, :, HEAD_DIM:] = turned_tangent
                outs[slot][1] = extra[other // 4]


def norm_rope(*operands):
    return call(
        norm_rope_kernel,
        "norm_rope",
        [shape(SLOT, 256)] * CHIPS + [shape(2, ROWS, 256)] * CHIPS,
        operands,
        [pltpu.VMEM((2, ROWS, 256), BF16)] * 2,
        60,
        cost(40 * ROWS * FEATURES, 5 * MIB),
        1,
    )


def attend_kernel(first, last, chunks, *refs):
    q_in = refs[:CHIPS]
    k_in = refs[CHIPS : CHIPS + chunks]
    v_in = refs[CHIPS + chunks : CHIPS + 2 * chunks]
    rest = refs[CHIPS + 2 * chunks :]
    before = None
    if not first:
        before, rest = rest[0], rest[1:]
    if last:
        outs, rest = rest[:CHIPS], rest[CHIPS:]
    else:
        state, rest = rest[0], rest[1:]
    queries, keys, values = rest[:3]
    for slot in range(CHIPS):
        queries[slot * ROWS : (slot + 1) * ROWS] = q_in[slot][:ROWS]
        low = CHIPS * ROWS + slot * PART
        queries[low : low + PART] = q_in[slot][ROWS:]
    for chunk in range(chunks):
        rows = slice(chunk * ROWS, (chunk + 1) * ROWS)
        for place in range(2):
            keys[place, rows] = k_in[chunk][place]
            values[place, rows] = v_in[chunk][place]
    tiles = CHIPS * SLOT // TILE_Q
    steps = chunks * ROWS // TILE_K

    def one_tile(tile, carry):
        place = tile // (tiles - 1)
        both = queries[pl.ds(pl.multiple_of(tile * TILE_Q, TILE_Q), TILE_Q)]
        plain = both[:, :HEAD_DIM]
        crossed = jnp.concatenate([both[:, HEAD_DIM:], plain], axis=1)
        if first:
            weighted = jnp.zeros((TILE_Q, 256), F32)
            weighted_tangent = jnp.zeros((TILE_Q, HEAD_DIM), F32)
        else:
            weighted = before[tile, :, :256]
            weighted_tangent = before[tile, :, 256:384]
        norm_lanes = jnp.zeros((TILE_Q, HEAD_DIM), F32)
        tangent_lanes = jnp.zeros((TILE_Q, HEAD_DIM), F32)
        for step in range(steps):
            rows = slice(step * TILE_K, (step + 1) * TILE_K)
            key_rows = keys[place, rows]
            value_rows = values[place, rows]
            scores = dot_rows(plain, key_rows[:, :HEAD_DIM])
            scores_tangent = dot_rows(crossed, key_rows)
            squashed = jnp.tanh(scores * (SCALE / CAP))
            weights = jnp.exp2(squashed * (CAP * math.log2(math.e)))
            weights_tangent = weights * ((1.0 - squashed * squashed) * scores_tangent)
            for low in range(0, TILE_K, HEAD_DIM):
                norm_lanes = norm_lanes + weights[:, low : low + HEAD_DIM]
                tangent_lanes = tangent_lanes + weights_tangent[:, low : low + HEAD_DIM]
            weighted = weighted + dot(weights.astype(BF16), value_rows)
            weighted_tangent = weighted_tangent + dot(
                weights_tangent.astype(BF16), value_rows[:, :HEAD_DIM]
            )
        norm_sum = jnp.sum(norm_lanes, axis=1, keepdims=True)
        tangent_sum = jnp.sum(tangent_lanes, axis=1, keepdims=True)
        if not first:
            norm_sum = norm_sum + before[tile, :, 384:385]
            tangent_sum = tangent_sum + before[tile, :, 448:449]
        if last:
            inverse = 1.0 / norm_sum
            attention = weighted[:, :HEAD_DIM] * inverse
            attention_tangent = (
                weighted[:, HEAD_DIM:] + weighted_tangent * SCALE
            ) * inverse - (tangent_sum * SCALE * inverse) * attention
            outcome = jnp.concatenate([attention, attention_tangent], axis=1)
            rest[3][pl.ds(pl.multiple_of(tile * TILE_Q, TILE_Q), TILE_Q)] = outcome.astype(BF16)
        else:
            state[tile, :, :256] = weighted
            state[tile, :, 256:384] = weighted_tangent
            state[tile, :, 384:448] = jnp.broadcast_to(norm_sum, (TILE_Q, 64))
            state[tile, :, 448:] = jnp.broadcast_to(tangent_sum, (TILE_Q, 64))
        return carry

    lax.fori_loop(0, tiles, one_tile, 0)
    if last:
        for slot in range(CHIPS):
            outs[slot][:ROWS] = rest[3][slot * ROWS : (slot + 1) * ROWS]
            low = CHIPS * ROWS + slot * PART
            outs[slot][ROWS:] = rest[3][low : low + PART]


def attend(queries, keys, values, before=None, last=False):
    chunks = len(keys)
    tiles = CHIPS * SLOT // TILE_Q
    first = before is None
    operands = list(queries) + list(keys) + list(values) + ([] if first else [before])
    outs = [shape(SLOT, 256)] * CHIPS if last else shape(tiles, TILE_Q, 512, kind=F32)
    scratch = [
        pltpu.VMEM((CHIPS * SLOT, 256), BF16),
        pltpu.VMEM((2, chunks * ROWS, 256), BF16),
        pltpu.VMEM((2, chunks * ROWS, 256), BF16),
    ]
    if last:
        scratch.append(pltpu.VMEM((CHIPS * SLOT, 256), BF16))
    return call(
        functools.partial(attend_kernel, first, last, chunks),
        "attend",
        outs,
        operands,
        scratch,
        60,
        cost(8 * 256 * CHIPS * SLOT * chunks * ROWS, 10 * MIB),
    )


def project_kernel(meta, *refs):
    parts = refs[:CHIPS]
    mine, theirs, out, left, right = refs[CHIPS:]
    chip = meta[0]
    core = meta[1]

    @pl.when(pl.program_id(0) == 0)
    def _():
        for slot in range(CHIPS):
            other = jnp.bitwise_xor(chip, slot)
            left[other, :ROWS] = parts[slot][:ROWS, :HEAD_DIM]
            left[other, ROWS:] = parts[slot][:ROWS, HEAD_DIM:]
            shared = CHIPS + other // 4
            start = pl.multiple_of(other % 4 * PART, 16)
            left[shared, pl.ds(start, PART)] = parts[slot][ROWS:, :HEAD_DIM]
            left[shared, pl.ds(ROWS + start, PART)] = parts[slot][ROWS:, HEAD_DIM:]

    half = FEATURES // 2
    right[pl.ds(pl.multiple_of(core * half, half), half)] = mine[0]
    right[pl.ds(pl.multiple_of((1 - core) * half, half), half)] = theirs[0]
    rows = jnp.concatenate([left[head] for head in range(HEADS)], axis=1)
    for low in range(0, FEATURES, 256):
        out[:, low : low + 256] = dot(rows, right[:, low : low + 256]).astype(out.dtype)


def project(meta, parts, mine, theirs, kind):
    half = FEATURES // 2

    def of_block(step, meta):
        return (2 * meta[2] + step, 0, 0)

    whole = pl.BlockSpec((SLOT, 256), lambda step, meta: (0, 0))
    return pl.pallas_call(
        project_kernel,
        out_shape=shape(2 * ROWS, 2 * FEATURES, kind=kind),
        grid_spec=pltpu.PrefetchScalarGridSpec(
            num_scalar_prefetch=1,
            grid=(2,),
            in_specs=[whole] * CHIPS
            + [pl.BlockSpec((1, half, FEATURES), of_block)] * 2,
            out_specs=pl.BlockSpec((2 * ROWS, FEATURES), lambda step, meta: (0, step)),
            scratch_shapes=[
                pltpu.VMEM((HEADS, 2 * ROWS, HEAD_DIM), BF16),
                pltpu.VMEM((FEATURES, FEATURES), BF16),
            ],
        ),
        compiler_params=params(60),
        cost_estimate=cost(2 * 2 * ROWS * FEATURES * 2 * FEATURES, 10 * MIB),
        name="project",
    )(meta, *parts, mine, theirs)


def to_chip(array, slot):
    if slot == 0:
        return array
    return lax.ppermute(array, "ctx", [(place, place ^ (2 * slot)) for place in range(16)])


def to_core(array):
    return lax.ppermute(array, "ctx", [(place, place ^ 1) for place in range(16)])


def to_group(array):
    return lax.ppermute(array, "head", [(0, 1), (1, 0)])


def on_device(
    query_input,
    key_input,
    value_input,
    query_tangent,
    key_tangent,
    value_tangent,
    query_gain,
    key_gain,
    out_weight,
    span_order,
):
    place = lax.axis_index("ctx")
    group = lax.axis_index("head")
    chip, core = place // 2, place % 2
    meta = jnp.stack([chip, core, group]).astype(jnp.int32)
    half = FEATURES // 2
    own_half = lax.dynamic_slice_in_dim(out_weight, core * half, half, 0)
    weight_mine = lax.all_gather(own_half, "dp", axis=0)

    raw = [
        member[0]
        for member in (
            query_input,
            query_tangent,
            key_input,
            key_tangent,
            value_input,
            value_tangent,
        )
    ]
    *value_slots, stats = prepare(meta, *raw)
    stats_peer = to_group(stats)
    order = (0, 1, 3, 4, 2, 5, 7, 6)
    cosine, sine = rope_tables(lax.dynamic_slice_in_dim(span_order, 2 * place, 2))
    slots = norm_rope(
        meta,
        *raw[:4],
        stats,
        stats_peer,
        query_gain[None],
        key_gain[None],
        cosine,
        sine,
    )
    value_slots[5:], slots = lax.optimization_barrier((value_slots[5:], slots))
    values = [to_chip(value_slots[slot], slot) for slot in order]
    queries = [to_chip(slots[slot], slot) for slot in range(CHIPS)]
    keys = [to_chip(slots[CHIPS + slot], slot) for slot in order]
    values = values + [to_core(member) for member in values]
    keys = keys + [to_core(member) for member in keys]
    early = [0, 1, 2, 3, 8, 9, 10, 11]
    late = [4, 5, 6, 7, 12, 13, 14, 15]
    state = attend(queries, [keys[i] for i in early], [values[i] for i in early])
    results = attend(
        queries, [keys[i] for i in late], [values[i] for i in late], state, last=True
    )
    weight_mine, results = lax.optimization_barrier((weight_mine, results))
    weight_theirs = to_core(weight_mine)
    parts = [to_chip(results[slot], slot) for slot in range(CHIPS)]
    for_peer = project(
        meta.at[2].set(1 - group), parts, weight_mine, weight_theirs, BF16
    )
    from_peer = to_group(for_peer)
    own = project(meta, parts, weight_mine, weight_theirs, F32)
    total = (own + from_peer.astype(F32)).astype(BF16)
    return (total[:ROWS][None], total[ROWS:][None])


def solution(mesh):
    return jax.shard_map(
        on_device,
        mesh=mesh,
        in_specs=(
            P("dp", "ctx", "head"),
            P("dp", "ctx", "head"),
            P("dp", "ctx", "head"),
            P("dp", "ctx", "head"),
            P("dp", "ctx", "head"),
            P("dp", "ctx", "head"),
            P("head"),
            P("head"),
            P("head", "dp"),
            P(),
        ),
        out_specs=(P("dp", "ctx", "head"), P("dp", "ctx", "head")),
        check_vma=False,
    )
```

```python
import functools
import math

import jax
import jax.numpy as jnp
from jax import lax
from jax.experimental import pallas as pl
from jax.experimental.pallas import tpu as pltpu
from jax.sharding import PartitionSpec as P

HEAD_DIM = 128
GRID_H = 8
GRID_W = 16
CAP = 30
HD = 2560
SPAN = 96
ROWS = 192
HEADS = 10
FEATURES = HEADS * HEAD_DIM
CHIPS = 8
PART = 48
SLOT = ROWS + PART
TILE_Q = 384
TILE_K = 768
SCALE = 1.0 / math.sqrt(HEAD_DIM)
BF16 = jnp.bfloat16
F32 = jnp.float32
MIB = 2**20
SMEM = pl.BlockSpec(memory_space=pltpu.SMEM)


def params(mib):
    return pltpu.CompilerParams(vmem_limit_bytes=mib * MIB)


def cost(flops, moved):
    return pl.CostEstimate(flops=flops, bytes_accessed=moved, transcendentals=0)


def shape(*dims, kind=BF16):
    return jax.ShapeDtypeStruct(dims, kind)


def whole(member):
    return pl.BlockSpec(member.shape, lambda step: (0,) * len(member.shape))


def call(kernel, name, outs, operands, scratch, mib, estimate, scalars=0):
    return pl.pallas_call(
        kernel,
        grid=(1,),
        out_shape=outs,
        in_specs=[SMEM] * scalars + [whole(member) for member in operands[scalars:]],
        out_specs=jax.tree.map(whole, outs),
        scratch_shapes=scratch,
        compiler_params=params(mib),
        cost_estimate=estimate,
        name=name,
    )(*operands)


def dot(left, right):
    return lax.dot_general(left, right, (((1,), (0,)), ((), ())), preferred_element_type=F32)


def dot_rows(left, right):
    return lax.dot_general(left, right, (((1,), (1,)), ((), ())), preferred_element_type=F32)


def rope_tables(own_spans):
    positions = (
        own_spans[:, None] * SPAN + jnp.arange(SPAN, dtype=jnp.int32)[None, :]
    ).reshape(-1)
    pairs = HEAD_DIM // 2
    side = pairs // 3
    time = pairs - 2 * side
    time_freq = 10000.0 ** (-jnp.arange(time, dtype=F32) / time)
    side_freq = 10000.0 ** (-jnp.arange(side, dtype=F32) / side)
    freq = jnp.concatenate([time_freq, side_freq, side_freq])
    freq = jnp.broadcast_to(freq[:, None], (pairs, 2)).reshape(1, HEAD_DIM)
    pair = (jnp.arange(HEAD_DIM, dtype=jnp.int32) // 2)[None, :]
    place = jnp.where(
        pair < time,
        (positions // (GRID_H * GRID_W))[:, None],
        jnp.where(
            pair < time + side,
            (positions // GRID_W % GRID_H)[:, None],
            (positions % GRID_W)[:, None],
        ),
    ).astype(F32)
    angle = place * freq
    return jnp.cos(angle), jnp.sin(angle)


def prepare_kernel(q, qt, k, kt, v, vt, out, stats):
    for chip in range(CHIPS):
        for place, head in ((0, chip), (1, CHIPS + chip // 4)):
            columns = slice(head * HEAD_DIM, (head + 1) * HEAD_DIM)
            out[chip, place, :, :HEAD_DIM] = v[:, columns]
            out[chip, place, :, HEAD_DIM:] = vt[:, columns]
    lane = lax.broadcasted_iota(jnp.int32, (ROWS, HEAD_DIM), 1)
    total = jnp.zeros((ROWS, HEAD_DIM), F32)
    for place, (left, right) in enumerate(((q, q), (q, qt), (k, k), (k, kt))):
        product = left[...].astype(F32) * right[...].astype(F32)
        total = jnp.where(lane == place, jnp.sum(product, axis=1, keepdims=True), total)
    stats[...] = total


def prepare(*operands):
    return call(
        prepare_kernel,
        "prepare",
        [shape(CHIPS, 2, ROWS, 256), shape(ROWS, HEAD_DIM, kind=F32)],
        operands,
        [],
        60,
        cost(8 * ROWS * FEATURES, 6 * MIB),
    )


def norm_rope_kernel(q, qt, k, kt, mine, theirs, q_gain, k_gain, cosine, sine, out):
    stats = mine[...] + theirs[...]
    cos = cosine[...]
    even = lax.broadcasted_iota(jnp.int32, (ROWS, HEAD_DIM), 1) % 2 == 0
    sin_next = jnp.where(even, -sine[...], 0.0)
    sin_last = jnp.where(even, 0.0, sine[...])

    def rotated(x):
        after = pltpu.roll(x, HEAD_DIM - 1, 1)
        before = pltpu.roll(x, 1, 1)
        return (x * cos + (after * sin_next + before * sin_last)).astype(BF16)

    def of_head(raw_ref, tangent_ref, gain_ref, inverse, mixing, head):
        columns = slice(head * HEAD_DIM, (head + 1) * HEAD_DIM)
        raw = raw_ref[:, columns].astype(F32)
        tangent = tangent_ref[:, columns].astype(F32)
        gain = gain_ref[:, columns]
        normed = gain * raw * inverse
        normed_tangent = gain * (
            tangent * inverse - raw * mixing * inverse * inverse * inverse
        )
        return rotated(normed), rotated(normed_tangent)

    wide = (ROWS, HEAD_DIM)
    for first, raw_ref, tangent_ref, gain_ref in ((2, k, kt, k_gain), (0, q, qt, q_gain)):
        inverse = jnp.broadcast_to(lax.rsqrt(stats[:, first : first + 1] / HD + 1e-06), wide)
        mixing = jnp.broadcast_to(stats[:, first + 1 : first + 2] / HD, wide)
        for head in range(HEADS):
            turned = jnp.concatenate(
                of_head(raw_ref, tangent_ref, gain_ref, inverse, mixing, head), axis=1
            )
            low = 0 if first else 2 * ROWS
            if head < CHIPS:
                out[head, low : low + ROWS] = turned
                continue
            for column in range(4):
                chip = 4 * (head - CHIPS) + column
                if first:
                    out[chip, ROWS : 2 * ROWS] = turned
                else:
                    out[chip, 3 * ROWS :] = turned[column * PART : (column + 1) * PART]


def norm_rope(*operands):
    return call(
        norm_rope_kernel,
        "norm_rope",
        [shape(CHIPS, 2 * ROWS + SLOT, 256)],
        operands,
        [],
        60,
        cost(40 * ROWS * FEATURES, 5 * MIB),
    )[0]


def attend_kernel(mixed, mixed_other, v_in, v_other, out, keys, values, queries, results, sems):
    copies = []

    def copy(source, target):
        copies.append(pltpu.make_async_copy(source, target, sems.at[len(copies)]))
        copies[-1].start()

    main = CHIPS * ROWS
    for chip in range(CHIPS):
        copy(mixed.at[chip, 2 * ROWS : 3 * ROWS], queries.at[chip * ROWS : (chip + 1) * ROWS])
        low = main + chip * PART
        copy(mixed.at[chip, 3 * ROWS :], queries.at[low : low + PART])
    asked = len(copies)
    for place in range(2):
        for chunk in range(2 * CHIPS):
            rows = slice(chunk * ROWS, (chunk + 1) * ROWS)
            k_from, v_from = ((mixed, v_in), (mixed_other, v_other))[chunk // CHIPS]
            chip = chunk % CHIPS
            copy(k_from.at[chip, place * ROWS : (place + 1) * ROWS], keys.at[place, rows])
            copy(v_from.at[chip, place], values.at[place, rows])
    per_step = 2 * TILE_K // ROWS
    steps = 2 * CHIPS * ROWS // TILE_K

    def one_tile(start, size, place, wait):
        both = queries[pl.ds(start, size)]
        plain = both[:, :HEAD_DIM]
        crossed = jnp.concatenate([both[:, HEAD_DIM:], plain], axis=1)
        weighted = jnp.zeros((size, 256), F32)
        weighted_tangent = jnp.zeros((size, HEAD_DIM), F32)
        norm_lanes = jnp.zeros((size, HEAD_DIM), F32)
        tangent_lanes = jnp.zeros((size, HEAD_DIM), F32)
        for step in range(steps):
            if wait:
                low = asked + (place * steps + step) * per_step
                for member in copies[low : low + per_step]:
                    member.wait()
            rows = slice(step * TILE_K, (step + 1) * TILE_K)
            key_rows = keys[place, rows]
            value_rows = values[place, rows]
            scores = dot_rows(plain, key_rows[:, :HEAD_DIM])
            scores_tangent = dot_rows(crossed, key_rows) * SCALE
            squashed = jnp.tanh(scores * (SCALE / CAP))
            weights = jnp.exp2(squashed * (CAP * math.log2(math.e)))
            weights_tangent = weights * ((1.0 - squashed * squashed) * scores_tangent)
            for low in range(0, TILE_K, HEAD_DIM):
                norm_lanes = norm_lanes + weights[:, low : low + HEAD_DIM]
                tangent_lanes = tangent_lanes + weights_tangent[:, low : low + HEAD_DIM]
            weighted = weighted + dot(weights.astype(BF16), value_rows)
            weighted_tangent = weighted_tangent + dot(
                weights_tangent.astype(BF16), value_rows[:, :HEAD_DIM]
            )
        inverse = 1.0 / jnp.sum(norm_lanes, axis=1, keepdims=True)
        shift = jnp.sum(tangent_lanes, axis=1, keepdims=True) * inverse
        attention = weighted[:, :HEAD_DIM] * inverse
        attention_tangent = (
            weighted[:, HEAD_DIM:] + weighted_tangent
        ) * inverse - shift * attention
        outcome = jnp.concatenate([attention, attention_tangent], axis=1)
        results[pl.ds(start, size)] = outcome.astype(BF16)

    for member in copies[:asked]:
        member.wait()
    one_tile(0, TILE_Q, 0, True)

    def later(tile, carry):
        one_tile(pl.multiple_of(tile * TILE_Q, TILE_Q), TILE_Q, 0, False)
        return carry

    lax.fori_loop(1, main // TILE_Q, later, 0)
    one_tile(main, CHIPS * PART, 1, True)
    for group in range(2):
        for chip in range(CHIPS):
            out[group, chip, :ROWS] = results[chip * ROWS : (chip + 1) * ROWS]
            low = main + chip * PART
            out[group, chip, ROWS:] = results[low : low + PART]


def attend(*operands):
    anywhere = pl.BlockSpec(memory_space=pl.ANY)
    outs = [shape(2, CHIPS, SLOT, 256)]
    return pl.pallas_call(
        attend_kernel,
        grid=(1,),
        out_shape=outs,
        in_specs=[anywhere] * len(operands),
        out_specs=jax.tree.map(whole, outs),
        scratch_shapes=[
            pltpu.VMEM((2, 2 * CHIPS * ROWS, 256), BF16),
            pltpu.VMEM((2, 2 * CHIPS * ROWS, 256), BF16),
            pltpu.VMEM((CHIPS * SLOT, 256), BF16),
            pltpu.VMEM((CHIPS * SLOT, 256), BF16),
            pltpu.SemaphoreType.DMA((10 * CHIPS,)),
        ],
        compiler_params=params(60),
        cost_estimate=cost(8 * 256 * CHIPS * SLOT * 2 * CHIPS * ROWS, 14 * MIB),
        name="attend",
    )(*operands)[0]


def project_kernel(meta, parts, *refs):
    pieces = refs[:6]
    out, out_tangent, left = refs[6:]

    @pl.when(pl.program_id(0) == 0)
    def _():
        for group in range(2):
            first = HEADS * jnp.bitwise_xor(group, meta[2])
            start = HEADS - meta[1] * (HEADS // 2)

            def column(head, first=first, start=start):
                return first + (head + start) % HEADS

            for chip in range(CHIPS):
                part = parts.at[group, chip]
                for side in range(2):
                    lanes = slice(side * HEAD_DIM, (side + 1) * HEAD_DIM)
                    top = side * ROWS
                    left[column(chip), top : top + ROWS] = part[:ROWS, lanes]
                    low = top + chip % 4 * PART
                    left[column(CHIPS + chip // 4), low : low + PART] = part[ROWS:, lanes]

    rows = jnp.concatenate([left[head] for head in range(2 * HEADS)], axis=1)
    for low in range(0, out.shape[1], 256):
        right = jnp.concatenate([piece[0, :, low : low + 256] for piece in pieces], axis=0)
        result = dot(rows, right).astype(out.dtype)
        out[:, low : low + 256] = result[:ROWS]
        out_tangent[:, low : low + 256] = result[ROWS:]


def project(meta, parts, own, cross):
    quarter = FEATURES // 4
    wide = FEATURES
    count = FEATURES // wide

    def straight(step, meta):
        return (2 * meta[2] + step // count, 0, step % count)

    def mirrored(step, meta):
        return (3 - 2 * meta[2] - step // count, 0, step % count)

    half_spec = pl.BlockSpec((1, 2 * quarter, wide), straight)
    quarter_specs = [pl.BlockSpec((1, quarter, wide), place) for place in (straight, mirrored)]
    out = shape(ROWS, 2 * FEATURES)
    out_spec = pl.BlockSpec((ROWS, wide), lambda step, meta: (0, step))
    return pl.pallas_call(
        project_kernel,
        out_shape=[out, out],
        grid_spec=pltpu.PrefetchScalarGridSpec(
            num_scalar_prefetch=1,
            grid=(2 * count,),
            in_specs=[pl.BlockSpec(parts.shape, lambda step, meta: (0, 0, 0, 0))]
            + [half_spec] * 2
            + quarter_specs * 2,
            out_specs=[out_spec, out_spec],
            scratch_shapes=[pltpu.VMEM((2 * HEADS, 2 * ROWS, HEAD_DIM), BF16)],
        ),
        compiler_params=params(60),
        cost_estimate=cost(2 * 2 * ROWS * 2 * FEATURES * 2 * FEATURES, 18 * MIB),
        name="project",
    )(meta, parts, *own, *[member for member in cross for _ in range(2)])


HOME = [(clip, group) for clip in range(4) for group in range(2) if clip // 2 == group]
AWAY = [(clip, group) for clip in range(4) for group in range(2) if clip // 2 != group]
CORES = [[2 * chip + core for chip in range(CHIPS)] for core in range(2)]
GROUP_CORES = [
    [16 * group + 2 * chip + core for group in range(2) for chip in range(CHIPS)]
    for core in range(2)
]


def to_chips(array):
    return lax.all_to_all(array, "ctx", 0, 0, axis_index_groups=CORES, tiled=True)


def to_core(array):
    return lax.ppermute(array, "ctx", [(place, place ^ 1) for place in range(16)])


def after(arrays, event):
    return lax.optimization_barrier((arrays, event))[0]


def move(array, pairs):
    pairs = [(2 * a + b, 2 * c + d) for (a, b), (c, d) in pairs]
    return lax.ppermute(array, ("dp", "head"), pairs)


def to_group(array):
    return lax.ppermute(array, "head", [(0, 1), (1, 0)])


def on_device(
    query_input,
    key_input,
    value_input,
    query_tangent,
    key_tangent,
    value_tangent,
    query_gain,
    key_gain,
    out_weight,
    span_order,
):
    place = lax.axis_index("ctx")
    group = lax.axis_index("head")
    chip, core = place // 2, place % 2
    meta = jnp.stack([chip, core, group]).astype(jnp.int32)
    half = FEATURES // 2
    own_rows = lax.dynamic_slice_in_dim(out_weight, core * half, half, 0)
    own_weight = lax.all_gather(own_rows, "dp", axis=0)

    raw = [
        member[0]
        for member in (
            query_input,
            query_tangent,
            key_input,
            key_tangent,
            value_input,
            value_tangent,
        )
    ]
    value_out, stats = prepare(*raw)
    values = to_chips(value_out)
    stats_peer = to_group(stats)
    cosine, sine = rope_tables(lax.dynamic_slice_in_dim(span_order, 2 * place, 2))
    gains = (query_gain[None], key_gain[None])
    values, stats_peer, cosine, sine, gains = lax.optimization_barrier(
        (values, stats_peer, cosine, sine, gains)
    )
    values_other = to_core(values)
    quarter = half // 2
    home = lax.axis_index("dp") // 2 == group
    lower, upper = [
        after(lax.dynamic_slice_in_dim(out_weight, core * half + low, quarter, 0), values)
        for low in (0, quarter)
    ]
    near = move(lower, [((clip, own), (clip, 1 - own)) for clip, own in AWAY])
    far = move(upper, [((clip, own), (3 - clip, 1 - own)) for clip, own in AWAY])
    mixed_out = norm_rope(*raw[:4], stats, stats_peer, *gains, cosine, sine)
    mixed = to_chips(after(mixed_out, values_other))
    near, far = after((near, far), mixed)
    cross_weight = lax.all_gather(jnp.where(home, near, far), "dp", axis=0)
    mixed_other = to_core(mixed)
    own_other = to_core(after(own_weight, mixed_other))
    results = attend(mixed, mixed_other, values, values_other)
    parts = lax.all_to_all(
        results.reshape(2 * CHIPS, SLOT, 256),
        ("head", "ctx"),
        0,
        0,
        axis_index_groups=GROUP_CORES,
        tiled=True,
    )
    cross_other = to_core(after(cross_weight, parts))
    projected, tangent = project(
        meta,
        parts.reshape(2, CHIPS, SLOT, 256),
        (own_weight, own_other),
        (cross_weight, cross_other),
    )
    return (projected[None], tangent[None])


def solution(mesh):
    return jax.shard_map(
        on_device,
        mesh=mesh,
        in_specs=(
            P("dp", "ctx", "head"),
            P("dp", "ctx", "head"),
            P("dp", "ctx", "head"),
            P("dp", "ctx", "head"),
            P("dp", "ctx", "head"),
            P("dp", "ctx", "head"),
            P("head"),
            P("head"),
            P("head", "dp"),
            P(),
        ),
        out_specs=(P("dp", "ctx", "head"), P("dp", "ctx", "head")),
        check_vma=False,
    )
```

```python
import functools
import math

import jax
import jax.numpy as jnp
from jax import lax
from jax.experimental import pallas as pl
from jax.experimental.pallas import tpu as pltpu
from jax.sharding import PartitionSpec as P

HEAD_DIM = 128
GRID_H = 8
GRID_W = 16
CAP = 30
HD = 2560
SPAN = 96
ROWS = 192
HEADS = 10
FEATURES = HEADS * HEAD_DIM
CHIPS = 8
PART = 48
SLOT = ROWS + PART
TILE_Q = 384
TILE_K = 256
SCALE = 1.0 / math.sqrt(HEAD_DIM)
BF16 = jnp.bfloat16
F32 = jnp.float32
MIB = 2**20
SMEM = pl.BlockSpec(memory_space=pltpu.SMEM)


def params(mib):
    return pltpu.CompilerParams(vmem_limit_bytes=mib * MIB)


def cost(flops, moved):
    return pl.CostEstimate(flops=flops, bytes_accessed=moved, transcendentals=0)


def shape(*dims, kind=BF16):
    return jax.ShapeDtypeStruct(dims, kind)


def whole(member):
    return pl.BlockSpec(member.shape, lambda step: (0,) * len(member.shape))


def call(kernel, name, outs, operands, scratch, mib, estimate, scalars=0):
    return pl.pallas_call(
        kernel,
        grid=(1,),
        out_shape=outs,
        in_specs=[SMEM] * scalars + [whole(member) for member in operands[scalars:]],
        out_specs=jax.tree.map(whole, outs),
        scratch_shapes=scratch,
        compiler_params=params(mib),
        cost_estimate=estimate,
        name=name,
    )(*operands)


def dot(left, right):
    return lax.dot_general(left, right, (((1,), (0,)), ((), ())), preferred_element_type=F32)


def dot_rows(left, right):
    return lax.dot_general(left, right, (((1,), (1,)), ((), ())), preferred_element_type=F32)


def rope_tables(own_spans):
    positions = (
        own_spans[:, None] * SPAN + jnp.arange(SPAN, dtype=jnp.int32)[None, :]
    ).reshape(-1)
    pairs = HEAD_DIM // 2
    side = pairs // 3
    time = pairs - 2 * side
    time_freq = 10000.0 ** (-jnp.arange(time, dtype=F32) / time)
    side_freq = 10000.0 ** (-jnp.arange(side, dtype=F32) / side)
    freq = jnp.concatenate([time_freq, side_freq, side_freq])
    freq = jnp.broadcast_to(freq[:, None], (pairs, 2)).reshape(1, HEAD_DIM)
    pair = (jnp.arange(HEAD_DIM, dtype=jnp.int32) // 2)[None, :]
    place = jnp.where(
        pair < time,
        (positions // (GRID_H * GRID_W))[:, None],
        jnp.where(
            pair < time + side,
            (positions // GRID_W % GRID_H)[:, None],
            (positions % GRID_W)[:, None],
        ),
    ).astype(F32)
    angle = place * freq
    return jnp.cos(angle), jnp.sin(angle)


def prepare_kernel(q, qt, k, kt, v, vt, out, stats):
    for chip in range(CHIPS):
        for place, head in ((0, chip), (1, CHIPS + chip // 4)):
            columns = slice(head * HEAD_DIM, (head + 1) * HEAD_DIM)
            out[chip, place, :, :HEAD_DIM] = v[:, columns]
            out[chip, place, :, HEAD_DIM:] = vt[:, columns]
    lane = lax.broadcasted_iota(jnp.int32, (ROWS, HEAD_DIM), 1)
    total = jnp.zeros((ROWS, HEAD_DIM), F32)
    for place, (left, right) in enumerate(((q, q), (q, qt), (k, k), (k, kt))):
        product = left[...].astype(F32) * right[...].astype(F32)
        total = jnp.where(lane == place, jnp.sum(product, axis=1, keepdims=True), total)
    stats[...] = total


def prepare(*operands):
    return call(
        prepare_kernel,
        "prepare",
        [shape(CHIPS, 2, ROWS, 256), shape(ROWS, HEAD_DIM, kind=F32)],
        operands,
        [],
        60,
        cost(8 * ROWS * FEATURES, 6 * MIB),
    )


def norm_rope_kernel(q, qt, k, kt, mine, theirs, q_gain, k_gain, cosine, sine, out):
    stats = mine[...] + theirs[...]
    cos = cosine[...]
    even = lax.broadcasted_iota(jnp.int32, (ROWS, HEAD_DIM), 1) % 2 == 0
    sin_next = jnp.where(even, -sine[...], 0.0)
    sin_last = jnp.where(even, 0.0, sine[...])

    def rotated(x):
        after = pltpu.roll(x, HEAD_DIM - 1, 1)
        before = pltpu.roll(x, 1, 1)
        return (x * cos + (after * sin_next + before * sin_last)).astype(BF16)

    def of_head(raw_ref, tangent_ref, gain_ref, inverse, mixing, head):
        columns = slice(head * HEAD_DIM, (head + 1) * HEAD_DIM)
        raw = raw_ref[:, columns].astype(F32)
        tangent = tangent_ref[:, columns].astype(F32)
        gain = gain_ref[:, columns]
        normed = gain * raw * inverse
        normed_tangent = gain * (
            tangent * inverse - raw * mixing * inverse * inverse * inverse
        )
        return rotated(normed), rotated(normed_tangent)

    wide = (ROWS, HEAD_DIM)
    for first, raw_ref, tangent_ref, gain_ref in ((2, k, kt, k_gain), (0, q, qt, q_gain)):
        inverse = jnp.broadcast_to(lax.rsqrt(stats[:, first : first + 1] / HD + 1e-06), wide)
        mixing = jnp.broadcast_to(stats[:, first + 1 : first + 2] / HD, wide)
        for head in range(HEADS):
            turned = jnp.concatenate(
                of_head(raw_ref, tangent_ref, gain_ref, inverse, mixing, head), axis=1
            )
            low = 0 if first else 2 * ROWS
            if head < CHIPS:
                out[head, low : low + ROWS] = turned
                continue
            for column in range(4):
                chip = 4 * (head - CHIPS) + column
                if first:
                    out[chip, ROWS : 2 * ROWS] = turned
                else:
                    out[chip, 3 * ROWS :] = turned[column * PART : (column + 1) * PART]


def norm_rope(*operands):
    return call(
        norm_rope_kernel,
        "norm_rope",
        [shape(CHIPS, 2 * ROWS + SLOT, 256)],
        operands,
        [],
        60,
        cost(40 * ROWS * FEATURES, 5 * MIB),
    )[0]


def attend_kernel(mixed, mixed_other, v_in, v_other, out, keys, values, queries, results, sems):
    copies = []

    def copy(source, target):
        copies.append(pltpu.make_async_copy(source, target, sems.at[len(copies)]))
        copies[-1].start()

    main = CHIPS * ROWS
    for chip in range(CHIPS):
        copy(mixed.at[chip, 2 * ROWS : 3 * ROWS], queries.at[chip * ROWS : (chip + 1) * ROWS])
        low = main + chip * PART
        copy(mixed.at[chip, 3 * ROWS :], queries.at[low : low + PART])
    asked = len(copies)
    for place in range(2):
        for chunk in range(2 * CHIPS):
            rows = slice(chunk * ROWS, (chunk + 1) * ROWS)
            k_from, v_from = ((mixed, v_in), (mixed_other, v_other))[chunk // CHIPS]
            chip = chunk % CHIPS
            copy(k_from.at[chip, place * ROWS : (place + 1) * ROWS], keys.at[place, rows])
            copy(v_from.at[chip, place], values.at[place, rows])
    steps = 2 * CHIPS * ROWS // TILE_K
    group = 3 * TILE_K
    per_group = 2 * group // ROWS

    def one_tile(start, size, place, wait):
        both = queries[pl.ds(start, size)]
        plain = both[:, :HEAD_DIM]
        crossed = jnp.concatenate([both[:, HEAD_DIM:], plain], axis=1)
        weighted = jnp.zeros((size, 256), F32)
        weighted_tangent = jnp.zeros((size, HEAD_DIM), F32)
        norm_lanes = jnp.zeros((size, HEAD_DIM), F32)
        tangent_lanes = jnp.zeros((size, HEAD_DIM), F32)

        def rows(step):
            return slice(step * TILE_K, (step + 1) * TILE_K)

        def score(step):
            if wait and step % 3 == 0:
                low = asked + (place * steps + step) // 3 * per_group
                for member in copies[low : low + per_group]:
                    member.wait()
            key_rows = keys[place, rows(step)]
            return dot_rows(plain, key_rows[:, :HEAD_DIM]), dot_rows(crossed, key_rows)

        ahead, behind = score(0), None
        for step in range(steps + 1):
            if step < steps:
                scores, scores_tangent = ahead
                if step + 1 < steps:
                    ahead = score(step + 1)
                squashed = jnp.tanh(scores * (SCALE / CAP))
                weights = jnp.exp2(squashed * (CAP * math.log2(math.e)))
                weights_tangent = weights * (
                    (1.0 - squashed * squashed) * (scores_tangent * SCALE)
                )
                for low in range(0, TILE_K, HEAD_DIM):
                    norm_lanes = norm_lanes + weights[:, low : low + HEAD_DIM]
                    tangent_lanes = tangent_lanes + weights_tangent[:, low : low + HEAD_DIM]
            if step > 0:
                value_rows = values[place, rows(step - 1)]
                weighted = weighted + dot(behind[0], value_rows)
                weighted_tangent = weighted_tangent + dot(behind[1], value_rows[:, :HEAD_DIM])
            behind = (weights.astype(BF16), weights_tangent.astype(BF16))
        inverse = 1.0 / jnp.sum(norm_lanes, axis=1, keepdims=True)
        shift = jnp.sum(tangent_lanes, axis=1, keepdims=True) * inverse
        attention = weighted[:, :HEAD_DIM] * inverse
        attention_tangent = (
            weighted[:, HEAD_DIM:] + weighted_tangent
        ) * inverse - shift * attention
        outcome = jnp.concatenate([attention, attention_tangent], axis=1)
        results[pl.ds(start, size)] = outcome.astype(BF16)

    for member in copies[:asked]:
        member.wait()
    one_tile(0, TILE_Q, 0, True)

    def later(tile, carry):
        one_tile(pl.multiple_of(tile * TILE_Q, TILE_Q), TILE_Q, 0, False)
        return carry

    lax.fori_loop(1, main // TILE_Q, later, 0)
    one_tile(main, CHIPS * PART, 1, True)
    for group in range(2):
        for chip in range(CHIPS):
            out[group, chip, :ROWS] = results[chip * ROWS : (chip + 1) * ROWS]
            low = main + chip * PART
            out[group, chip, ROWS:] = results[low : low + PART]


def attend(*operands):
    anywhere = pl.BlockSpec(memory_space=pl.ANY)
    outs = [shape(2, CHIPS, SLOT, 256)]
    return pl.pallas_call(
        attend_kernel,
        grid=(1,),
        out_shape=outs,
        in_specs=[anywhere] * len(operands),
        out_specs=jax.tree.map(whole, outs),
        scratch_shapes=[
            pltpu.VMEM((2, 2 * CHIPS * ROWS, 256), BF16),
            pltpu.VMEM((2, 2 * CHIPS * ROWS, 256), BF16),
            pltpu.VMEM((CHIPS * SLOT, 256), BF16),
            pltpu.VMEM((CHIPS * SLOT, 256), BF16),
            pltpu.SemaphoreType.DMA((10 * CHIPS,)),
        ],
        compiler_params=params(60),
        cost_estimate=cost(8 * 256 * CHIPS * SLOT * 2 * CHIPS * ROWS, 14 * MIB),
        name="attend",
    )(*operands)[0]


def project_kernel(last, meta, parts, *refs):
    pieces, refs = refs[:4], refs[4:]
    before, refs = (refs[0], refs[1:]) if last else (None, refs)
    outs, left = refs[:-1], refs[-1]

    @pl.when(pl.program_id(0) == 0)
    def _():
        def column(head):
            return (head + HEADS - meta[1] * (HEADS // 2)) % HEADS

        for chip in range(CHIPS):
            part = parts.at[0, chip]
            for side in range(2):
                lanes = slice(side * HEAD_DIM, (side + 1) * HEAD_DIM)
                top = side * ROWS
                left[column(chip), top : top + ROWS] = part[:ROWS, lanes]
                low = top + chip % 4 * PART
                left[column(CHIPS + chip // 4), low : low + PART] = part[ROWS:, lanes]

    rows = jnp.concatenate([left[head] for head in range(HEADS)], axis=1)
    for low in range(0, FEATURES, 256):
        columns = slice(low, low + 256)
        right = jnp.concatenate([piece[0, :, columns] for piece in pieces], axis=0)
        result = dot(rows, right)
        if last:
            result = result + before[:, columns]
            outs[0][:, columns] = result[:ROWS].astype(BF16)
            outs[1][:, columns] = result[ROWS:].astype(BF16)
        else:
            outs[0][:, columns] = result


def project(meta, parts, weights, before=None):
    last = before is not None
    quarter = FEATURES // 4

    def straight(step, meta):
        return (2 * meta[2] + step, 0, 0)

    def mirrored(step, meta):
        return (3 - 2 * meta[2] - step, 0, 0)

    def of_group(step, meta):
        return (1 - meta[2] if last else meta[2], 0, 0, 0)

    def columns(rows):
        return pl.BlockSpec((rows, FEATURES), lambda step, meta: (0, step))

    specs = [pl.BlockSpec((1, CHIPS, SLOT, 256), of_group)]
    specs += [pl.BlockSpec((1, quarter, FEATURES), at) for at in (straight, mirrored)] * 2
    operands = [member for member in weights for _ in range(2)]
    if last:
        operands += [before]
        specs += [columns(2 * ROWS)]
        outs, out_specs = [shape(ROWS, 2 * FEATURES)] * 2, [columns(ROWS)] * 2
    else:
        outs, out_specs = [shape(2 * ROWS, 2 * FEATURES, kind=F32)], [columns(2 * ROWS)]
    return pl.pallas_call(
        functools.partial(project_kernel, last),
        out_shape=outs,
        grid_spec=pltpu.PrefetchScalarGridSpec(
            num_scalar_prefetch=1,
            grid=(2,),
            in_specs=specs,
            out_specs=out_specs,
            scratch_shapes=[pltpu.VMEM((HEADS, 2 * ROWS, HEAD_DIM), BF16)],
        ),
        compiler_params=params(60),
        cost_estimate=cost(2 * 2 * ROWS * FEATURES * 2 * FEATURES, 12 * MIB),
        name="project",
    )(meta, parts, *operands)


HOME = [(clip, group) for clip in range(4) for group in range(2) if clip // 2 == group]
AWAY = [(clip, group) for clip in range(4) for group in range(2) if clip // 2 != group]
CORES = [[2 * chip + core for chip in range(CHIPS)] for core in range(2)]
GROUP_CORES = [
    [16 * group + 2 * chip + core for group in range(2) for chip in range(CHIPS)]
    for core in range(2)
]


def to_chips(array):
    return lax.all_to_all(array, "ctx", 0, 0, axis_index_groups=CORES, tiled=True)


def to_core(array):
    return lax.ppermute(array, "ctx", [(place, place ^ 1) for place in range(16)])


def after(arrays, event):
    return lax.optimization_barrier((arrays, event))[0]


def move(array, pairs):
    links = []
    for (clip, group), (next_clip, next_group) in pairs:
        flip = 8 * (group ^ next_group)
        for place in range(16):
            source = 32 * clip + 16 * group + place
            links.append((source, 32 * next_clip + 16 * next_group + (place ^ flip)))
    return lax.ppermute(array, ("dp", "head", "ctx"), links)


def to_group(array):
    return lax.ppermute(array, "head", [(0, 1), (1, 0)])


def on_device(
    query_input,
    key_input,
    value_input,
    query_tangent,
    key_tangent,
    value_tangent,
    query_gain,
    key_gain,
    out_weight,
    span_order,
):
    place = lax.axis_index("ctx")
    group = lax.axis_index("head")
    chip, core = place // 2, place % 2
    meta = jnp.stack([chip, core, group]).astype(jnp.int32)
    raw = [
        member[0]
        for member in (
            query_input,
            query_tangent,
            key_input,
            key_tangent,
            value_input,
            value_tangent,
        )
    ]
    quarter = FEATURES // 4
    home = lax.axis_index("dp") // 2 == group
    lower, upper = [
        lax.dynamic_slice_in_dim(out_weight, (2 * core + part) * quarter, quarter, 0)
        for part in range(2)
    ]
    second = move(upper, [((clip, own), (3 - clip, own)) for clip, own in HOME])
    value_out, stats = prepare(*raw)
    values = to_chips(value_out)
    stats_peer = to_group(stats)
    second, stats_peer = lax.optimization_barrier((second, stats_peer))
    cosine, sine = rope_tables(lax.dynamic_slice_in_dim(span_order, 2 * place, 2))
    gains = (query_gain[None], key_gain[None])
    values, stats_peer, cosine, sine, gains = lax.optimization_barrier(
        (values, stats_peer, cosine, sine, gains)
    )
    own_piece = jnp.where(home, lower, second)
    own_weight = lax.all_gather(own_piece, "dp", axis=0)
    values_other = to_core(values)
    near = move(after(lower, values), [((clip, own), (clip, 1 - own)) for clip, own in AWAY])
    far = move(after(upper, values), [((clip, own), (3 - clip, 1 - own)) for clip, own in AWAY])
    mixed_out = norm_rope(*raw[:4], stats, stats_peer, *gains, cosine, sine)
    mixed = to_chips(after(mixed_out, values_other))
    near, far = after((near, far), mixed)
    cross_weight = lax.all_gather(jnp.where(home, near, far), "dp", axis=0)
    mixed_other = to_core(mixed)
    own_other = to_core(after(own_weight, mixed_other))
    results = attend(mixed, mixed_other, values, values_other)
    parts = lax.all_to_all(
        results.reshape(2 * CHIPS, SLOT, 256),
        ("head", "ctx"),
        0,
        0,
        axis_index_groups=GROUP_CORES,
        tiled=True,
    )
    cross_other = to_core(after(cross_weight, parts))
    parts = parts.reshape(2, CHIPS, SLOT, 256)
    own = project(meta, parts, (own_weight, own_other))[0]
    projected, tangent = project(meta, parts, (cross_weight, cross_other), own)
    return (projected[None], tangent[None])


def solution(mesh):
    return jax.shard_map(
        on_device,
        mesh=mesh,
        in_specs=(
            P("dp", "ctx", "head"),
            P("dp", "ctx", "head"),
            P("dp", "ctx", "head"),
            P("dp", "ctx", "head"),
            P("dp", "ctx", "head"),
            P("dp", "ctx", "head"),
            P("head"),
            P("head"),
            P("head", "dp"),
            P(),
        ),
        out_specs=(P("dp", "ctx", "head"), P("dp", "ctx", "head")),
        check_vma=False,
    )
```

```python
import functools
import math

import jax
import jax.numpy as jnp
from jax import lax
from jax.experimental import pallas as pl
from jax.experimental.pallas import tpu as pltpu
from jax.sharding import PartitionSpec as P

HEAD_DIM = 128
GRID_H = 8
GRID_W = 16
CAP = 30
HD = 2560
SPAN = 96
ROWS = 192
HEADS = 10
FEATURES = HEADS * HEAD_DIM
CHIPS = 8
PART = 48
SLOT = ROWS + PART
TILE_Q = 384
TILE_K = 256
SCALE = 1.0 / math.sqrt(HEAD_DIM)
BF16 = jnp.bfloat16
F32 = jnp.float32
MIB = 2**20
SMEM = pl.BlockSpec(memory_space=pltpu.SMEM)


def params(mib):
    return pltpu.CompilerParams(vmem_limit_bytes=mib * MIB)


def cost(flops, moved):
    return pl.CostEstimate(flops=flops, bytes_accessed=moved, transcendentals=0)


def shape(*dims, kind=BF16):
    return jax.ShapeDtypeStruct(dims, kind)


def whole(member):
    return pl.BlockSpec(member.shape, lambda step: (0,) * len(member.shape))


def call(kernel, name, outs, operands, scratch, mib, estimate, scalars=0):
    return pl.pallas_call(
        kernel,
        grid=(1,),
        out_shape=outs,
        in_specs=[SMEM] * scalars + [whole(member) for member in operands[scalars:]],
        out_specs=jax.tree.map(whole, outs),
        scratch_shapes=scratch,
        compiler_params=params(mib),
        cost_estimate=estimate,
        name=name,
    )(*operands)


def dot(left, right):
    return lax.dot_general(left, right, (((1,), (0,)), ((), ())), preferred_element_type=F32)


def dot_rows(left, right):
    return lax.dot_general(left, right, (((1,), (1,)), ((), ())), preferred_element_type=F32)


def rope_tables(own_spans):
    positions = (
        own_spans[:, None] * SPAN + jnp.arange(SPAN, dtype=jnp.int32)[None, :]
    ).reshape(-1)
    pairs = HEAD_DIM // 2
    side = pairs // 3
    time = pairs - 2 * side
    time_freq = 10000.0 ** (-jnp.arange(time, dtype=F32) / time)
    side_freq = 10000.0 ** (-jnp.arange(side, dtype=F32) / side)
    freq = jnp.concatenate([time_freq, side_freq, side_freq])
    freq = jnp.broadcast_to(freq[:, None], (pairs, 2)).reshape(1, HEAD_DIM)
    pair = (jnp.arange(HEAD_DIM, dtype=jnp.int32) // 2)[None, :]
    place = jnp.where(
        pair < time,
        (positions // (GRID_H * GRID_W))[:, None],
        jnp.where(
            pair < time + side,
            (positions // GRID_W % GRID_H)[:, None],
            (positions % GRID_W)[:, None],
        ),
    ).astype(F32)
    angle = place * freq
    return jnp.cos(angle), jnp.sin(angle)


def prepare_kernel(q, qt, k, kt, v, vt, out, stats):
    for chip in range(CHIPS):
        for place, head in ((0, chip), (1, CHIPS + chip // 4)):
            columns = slice(head * HEAD_DIM, (head + 1) * HEAD_DIM)
            out[chip, place, :, :HEAD_DIM] = v[:, columns]
            out[chip, place, :, HEAD_DIM:] = vt[:, columns]
    lane = lax.broadcasted_iota(jnp.int32, (ROWS, HEAD_DIM), 1)
    total = jnp.zeros((ROWS, HEAD_DIM), F32)
    for place, (left, right) in enumerate(((q, q), (q, qt), (k, k), (k, kt))):
        product = left[...].astype(F32) * right[...].astype(F32)
        total = jnp.where(lane == place, jnp.sum(product, axis=1, keepdims=True), total)
    stats[...] = total


def prepare(*operands):
    return call(
        prepare_kernel,
        "prepare",
        [shape(CHIPS, 2, ROWS, 256), shape(ROWS, HEAD_DIM, kind=F32)],
        operands,
        [],
        60,
        cost(8 * ROWS * FEATURES, 6 * MIB),
    )


def norm_rope_kernel(q, qt, k, kt, mine, theirs, q_gain, k_gain, cosine, sine, out):
    stats = mine[...] + theirs[...]
    cos = cosine[...]
    even = lax.broadcasted_iota(jnp.int32, (ROWS, HEAD_DIM), 1) % 2 == 0
    sin_next = jnp.where(even, -sine[...], 0.0)
    sin_last = jnp.where(even, 0.0, sine[...])

    def rotated(x):
        after = pltpu.roll(x, HEAD_DIM - 1, 1)
        before = pltpu.roll(x, 1, 1)
        return (x * cos + (after * sin_next + before * sin_last)).astype(BF16)

    def of_head(raw_ref, tangent_ref, gain_ref, inverse, mixing, head):
        columns = slice(head * HEAD_DIM, (head + 1) * HEAD_DIM)
        raw = raw_ref[:, columns].astype(F32)
        tangent = tangent_ref[:, columns].astype(F32)
        gain = gain_ref[:, columns]
        normed = gain * raw * inverse
        normed_tangent = gain * (
            tangent * inverse - raw * mixing * inverse * inverse * inverse
        )
        return rotated(normed), rotated(normed_tangent)

    wide = (ROWS, HEAD_DIM)
    for first, raw_ref, tangent_ref, gain_ref in ((2, k, kt, k_gain), (0, q, qt, q_gain)):
        inverse = jnp.broadcast_to(lax.rsqrt(stats[:, first : first + 1] / HD + 1e-06), wide)
        mixing = jnp.broadcast_to(stats[:, first + 1 : first + 2] / HD, wide)
        for head in range(HEADS):
            turned = jnp.concatenate(
                of_head(raw_ref, tangent_ref, gain_ref, inverse, mixing, head), axis=1
            )
            low = 0 if first else 2 * ROWS
            if head < CHIPS:
                out[head, low : low + ROWS] = turned
                continue
            for column in range(4):
                chip = 4 * (head - CHIPS) + column
                if first:
                    out[chip, ROWS : 2 * ROWS] = turned
                else:
                    out[chip, 3 * ROWS :] = turned[column * PART : (column + 1) * PART]


def norm_rope(*operands):
    return call(
        norm_rope_kernel,
        "norm_rope",
        [shape(CHIPS, 2 * ROWS + SLOT, 256)],
        operands,
        [],
        60,
        cost(40 * ROWS * FEATURES, 5 * MIB),
    )[0]


def attend_kernel(mixed, mixed_other, v_in, v_other, out, keys, values, queries, results, sems):
    copies = []

    def copy(source, target):
        copies.append(pltpu.make_async_copy(source, target, sems.at[len(copies)]))
        copies[-1].start()

    main = CHIPS * ROWS
    for chip in range(CHIPS):
        copy(mixed.at[chip, 2 * ROWS : 3 * ROWS], queries.at[chip * ROWS : (chip + 1) * ROWS])
        low = main + chip * PART
        copy(mixed.at[chip, 3 * ROWS :], queries.at[low : low + PART])
    asked = len(copies)
    for place in range(2):
        for chunk in range(2 * CHIPS):
            rows = slice(chunk * ROWS, (chunk + 1) * ROWS)
            k_from, v_from = ((mixed, v_in), (mixed_other, v_other))[chunk // CHIPS]
            chip = chunk % CHIPS
            copy(k_from.at[chip, place * ROWS : (place + 1) * ROWS], keys.at[place, rows])
            copy(v_from.at[chip, place], values.at[place, rows])
    steps = 2 * CHIPS * ROWS // TILE_K
    group = 3 * TILE_K
    per_group = 2 * group // ROWS

    def one_tile(start, size, place, wait):
        both = queries[pl.ds(start, size)]
        plain = both[:, :HEAD_DIM]
        crossed = jnp.concatenate([both[:, HEAD_DIM:], plain], axis=1)
        weighted = jnp.zeros((size, 256), F32)
        weighted_tangent = jnp.zeros((size, HEAD_DIM), F32)
        norm_lanes = jnp.zeros((size, HEAD_DIM), F32)
        tangent_lanes = jnp.zeros((size, HEAD_DIM), F32)

        def rows(step):
            return slice(step * TILE_K, (step + 1) * TILE_K)

        def score(step):
            if wait and step % 3 == 0:
                low = asked + (place * steps + step) // 3 * per_group
                for member in copies[low : low + per_group]:
                    member.wait()
            key_rows = keys[place, rows(step)]
            return dot_rows(plain, key_rows[:, :HEAD_DIM]), dot_rows(crossed, key_rows)

        ahead, behind = score(0), None
        for step in range(steps + 1):
            if step < steps:
                scores, scores_tangent = ahead
                if step + 1 < steps:
                    ahead = score(step + 1)
                squashed = jnp.tanh(scores * (SCALE / CAP))
                weights = jnp.exp2(squashed * (CAP * math.log2(math.e)))
                weights_tangent = weights * (
                    (1.0 - squashed * squashed) * (scores_tangent * SCALE)
                )
                for low in range(0, TILE_K, HEAD_DIM):
                    norm_lanes = norm_lanes + weights[:, low : low + HEAD_DIM]
                    tangent_lanes = tangent_lanes + weights_tangent[:, low : low + HEAD_DIM]
            if step > 0:
                value_rows = values[place, rows(step - 1)]
                weighted = weighted + dot(behind[0], value_rows)
                weighted_tangent = weighted_tangent + dot(behind[1], value_rows[:, :HEAD_DIM])
            behind = (weights.astype(BF16), weights_tangent.astype(BF16))
        inverse = 1.0 / jnp.sum(norm_lanes, axis=1, keepdims=True)
        shift = jnp.sum(tangent_lanes, axis=1, keepdims=True) * inverse
        attention = weighted[:, :HEAD_DIM] * inverse
        attention_tangent = (
            weighted[:, HEAD_DIM:] + weighted_tangent
        ) * inverse - shift * attention
        outcome = jnp.concatenate([attention, attention_tangent], axis=1)
        results[pl.ds(start, size)] = outcome.astype(BF16)

    for member in copies[:asked]:
        member.wait()
    one_tile(0, TILE_Q, 0, True)

    def later(tile, carry):
        one_tile(pl.multiple_of(tile * TILE_Q, TILE_Q), TILE_Q, 0, False)
        return carry

    lax.fori_loop(1, main // TILE_Q, later, 0)
    one_tile(main, CHIPS * PART, 1, True)
    for group in range(2):
        for chip in range(CHIPS):
            out[group, chip, :ROWS] = results[chip * ROWS : (chip + 1) * ROWS]
            low = main + chip * PART
            out[group, chip, ROWS:] = results[low : low + PART]


def attend(*operands):
    anywhere = pl.BlockSpec(memory_space=pl.ANY)
    outs = [shape(2, CHIPS, SLOT, 256)]
    return pl.pallas_call(
        attend_kernel,
        grid=(1,),
        out_shape=outs,
        in_specs=[anywhere] * len(operands),
        out_specs=jax.tree.map(whole, outs),
        scratch_shapes=[
            pltpu.VMEM((2, 2 * CHIPS * ROWS, 256), BF16),
            pltpu.VMEM((2, 2 * CHIPS * ROWS, 256), BF16),
            pltpu.VMEM((CHIPS * SLOT, 256), BF16),
            pltpu.VMEM((CHIPS * SLOT, 256), BF16),
            pltpu.SemaphoreType.DMA((10 * CHIPS,)),
        ],
        compiler_params=params(60),
        cost_estimate=cost(8 * 256 * CHIPS * SLOT * 2 * CHIPS * ROWS, 14 * MIB),
        name="attend",
    )(*operands)[0]


def project_kernel(last, meta, parts, *refs):
    pieces, refs = refs[:4], refs[4:]
    before, refs = (refs[0], refs[1:]) if last else (None, refs)
    outs, left = refs[:-1], refs[-1]

    @pl.when(pl.program_id(0) == 0)
    def _():
        def column(head):
            return (head + HEADS - meta[1] * (HEADS // 2)) % HEADS

        for chip in range(CHIPS):
            part = parts.at[0, chip]
            for side in range(2):
                lanes = slice(side * HEAD_DIM, (side + 1) * HEAD_DIM)
                top = side * ROWS
                left[column(chip), top : top + ROWS] = part[:ROWS, lanes]
                low = top + chip % 4 * PART
                left[column(CHIPS + chip // 4), low : low + PART] = part[ROWS:, lanes]

    rows = jnp.concatenate([left[head] for head in range(HEADS)], axis=1)
    for low in range(0, FEATURES, 256):
        columns = slice(low, low + 256)
        right = jnp.concatenate([piece[0, :, columns] for piece in pieces], axis=0)
        result = dot(rows, right)
        if last:
            result = result + before[:, columns]
            outs[0][:, columns] = result[:ROWS].astype(BF16)
            outs[1][:, columns] = result[ROWS:].astype(BF16)
        else:
            outs[0][:, columns] = result


def project(meta, parts, weights, before=None):
    last = before is not None
    quarter = FEATURES // 4

    def straight(step, meta):
        return (2 * meta[2] + step, 0, 0)

    def mirrored(step, meta):
        return (3 - 2 * meta[2] - step, 0, 0)

    def of_group(step, meta):
        return (1 - meta[2] if last else meta[2], 0, 0, 0)

    def columns(rows):
        return pl.BlockSpec((rows, FEATURES), lambda step, meta: (0, step))

    specs = [pl.BlockSpec((1, CHIPS, SLOT, 256), of_group)]
    specs += [pl.BlockSpec((1, quarter, FEATURES), at) for at in (straight, mirrored)] * 2
    operands = [member for member in weights for _ in range(2)]
    if last:
        operands += [before]
        specs += [columns(2 * ROWS)]
        outs, out_specs = [shape(ROWS, 2 * FEATURES)] * 2, [columns(ROWS)] * 2
    else:
        outs, out_specs = [shape(2 * ROWS, 2 * FEATURES, kind=F32)], [columns(2 * ROWS)]
    return pl.pallas_call(
        functools.partial(project_kernel, last),
        out_shape=outs,
        grid_spec=pltpu.PrefetchScalarGridSpec(
            num_scalar_prefetch=1,
            grid=(2,),
            in_specs=specs,
            out_specs=out_specs,
            scratch_shapes=[pltpu.VMEM((HEADS, 2 * ROWS, HEAD_DIM), BF16)],
        ),
        compiler_params=params(60),
        cost_estimate=cost(2 * 2 * ROWS * FEATURES * 2 * FEATURES, 12 * MIB),
        name="project",
    )(meta, parts, *operands)


HOME = [(clip, group) for clip in range(4) for group in range(2) if clip // 2 == group]
AWAY = [(clip, group) for clip in range(4) for group in range(2) if clip // 2 != group]
CORES = [[2 * chip + core for chip in range(CHIPS)] for core in range(2)]
GROUP_CORES = [
    [16 * group + 2 * chip + core for group in range(2) for chip in range(CHIPS)]
    for core in range(2)
]


def to_chips(array):
    return lax.all_to_all(array, "ctx", 0, 0, axis_index_groups=CORES, tiled=True)


def to_core(array):
    return lax.ppermute(array, "ctx", [(place, place ^ 1) for place in range(16)])


def after(arrays, event):
    return lax.optimization_barrier((arrays, event))[0]


def move(array, pairs):
    links = []
    for (clip, group), (next_clip, next_group) in pairs:
        flip = 8 * (group ^ next_group)
        for place in range(16):
            source = 32 * clip + 16 * group + place
            links.append((source, 32 * next_clip + 16 * next_group + (place ^ flip)))
    return lax.ppermute(array, ("dp", "head", "ctx"), links)


def to_group(array):
    return lax.ppermute(array, "head", [(0, 1), (1, 0)])


def on_device(
    query_input,
    key_input,
    value_input,
    query_tangent,
    key_tangent,
    value_tangent,
    query_gain,
    key_gain,
    out_weight,
    span_order,
):
    place = lax.axis_index("ctx")
    group = lax.axis_index("head")
    chip, core = place // 2, place % 2
    meta = jnp.stack([chip, core, group]).astype(jnp.int32)
    raw = [
        member[0]
        for member in (
            query_input,
            query_tangent,
            key_input,
            key_tangent,
            value_input,
            value_tangent,
        )
    ]
    quarter = FEATURES // 4
    home = lax.axis_index("dp") // 2 == group
    lower, upper = [
        lax.dynamic_slice_in_dim(out_weight, (2 * core + part) * quarter, quarter, 0)
        for part in range(2)
    ]
    value_out, stats = prepare(*raw)
    second = move(after(upper, stats), [((clip, own), (3 - clip, own)) for clip, own in HOME])
    values = to_chips(value_out)
    stats_peer = to_group(stats)
    second, stats_peer = lax.optimization_barrier((second, stats_peer))
    cosine, sine = rope_tables(lax.dynamic_slice_in_dim(span_order, 2 * place, 2))
    gains = (query_gain[None], key_gain[None])
    values, stats_peer, cosine, sine, gains = lax.optimization_barrier(
        (values, stats_peer, cosine, sine, gains)
    )
    own_piece = jnp.where(home, lower, second)
    own_weight = lax.all_gather(own_piece, "dp", axis=0)
    values_other = to_core(values)
    near = move(after(lower, values), [((clip, own), (clip, 1 - own)) for clip, own in AWAY])
    far = move(after(upper, values), [((clip, own), (3 - clip, 1 - own)) for clip, own in AWAY])
    mixed_out = norm_rope(*raw[:4], stats, stats_peer, *gains, cosine, sine)
    mixed = to_chips(after(mixed_out, values_other))
    near, far = after((near, far), mixed)
    cross_weight = lax.all_gather(jnp.where(home, near, far), "dp", axis=0)
    mixed_other = to_core(mixed)
    own_other = to_core(after(own_weight, mixed_other))
    results = attend(mixed, mixed_other, values, values_other)
    parts = lax.all_to_all(
        results.reshape(2 * CHIPS, SLOT, 256),
        ("head", "ctx"),
        0,
        0,
        axis_index_groups=GROUP_CORES,
        tiled=True,
    )
    cross_other = to_core(after(cross_weight, parts))
    parts = parts.reshape(2, CHIPS, SLOT, 256)
    own = project(meta, parts, (own_weight, own_other))[0]
    projected, tangent = project(meta, parts, (cross_weight, cross_other), own)
    return (projected[None], tangent[None])


def solution(mesh):
    return jax.shard_map(
        on_device,
        mesh=mesh,
        in_specs=(
            P("dp", "ctx", "head"),
            P("dp", "ctx", "head"),
            P("dp", "ctx", "head"),
            P("dp", "ctx", "head"),
            P("dp", "ctx", "head"),
            P("dp", "ctx", "head"),
            P("head"),
            P("head"),
            P("head", "dp"),
            P(),
        ),
        out_specs=(P("dp", "ctx", "head"), P("dp", "ctx", "head")),
        check_vma=False,
    )
```

```python
import functools
import math

import jax
import jax.numpy as jnp
from jax import lax
from jax.experimental import pallas as pl
from jax.experimental.pallas import tpu as pltpu
from jax.sharding import PartitionSpec as P

HEAD_DIM = 128
GRID_H = 8
GRID_W = 16
CAP = 30
HD = 2560
SPAN = 96
ROWS = 192
HEADS = 10
FEATURES = HEADS * HEAD_DIM
CHIPS = 8
PART = 48
SLOT = ROWS + PART
TILE_Q = 384
TILE_K = 256
SCALE = 1.0 / math.sqrt(HEAD_DIM)
BF16 = jnp.bfloat16
F32 = jnp.float32
MIB = 2**20
SMEM = pl.BlockSpec(memory_space=pltpu.SMEM)


def params(mib):
    return pltpu.CompilerParams(vmem_limit_bytes=mib * MIB)


def cost(flops, moved):
    return pl.CostEstimate(flops=flops, bytes_accessed=moved, transcendentals=0)


def shape(*dims, kind=BF16):
    return jax.ShapeDtypeStruct(dims, kind)


def whole(member):
    return pl.BlockSpec(member.shape, lambda step: (0,) * len(member.shape))


def call(kernel, name, outs, operands, scratch, mib, estimate, scalars=0):
    return pl.pallas_call(
        kernel,
        grid=(1,),
        out_shape=outs,
        in_specs=[SMEM] * scalars + [whole(member) for member in operands[scalars:]],
        out_specs=jax.tree.map(whole, outs),
        scratch_shapes=scratch,
        compiler_params=params(mib),
        cost_estimate=estimate,
        name=name,
    )(*operands)


def dot(left, right):
    return lax.dot_general(left, right, (((1,), (0,)), ((), ())), preferred_element_type=F32)


def dot_rows(left, right):
    return lax.dot_general(left, right, (((1,), (1,)), ((), ())), preferred_element_type=F32)


def rope_tables(own_spans):
    positions = (
        own_spans[:, None] * SPAN + jnp.arange(SPAN, dtype=jnp.int32)[None, :]
    ).reshape(-1)
    pairs = HEAD_DIM // 2
    side = pairs // 3
    time = pairs - 2 * side
    time_freq = 10000.0 ** (-jnp.arange(time, dtype=F32) / time)
    side_freq = 10000.0 ** (-jnp.arange(side, dtype=F32) / side)
    freq = jnp.concatenate([time_freq, side_freq, side_freq])
    freq = jnp.broadcast_to(freq[:, None], (pairs, 2)).reshape(1, HEAD_DIM)
    pair = (jnp.arange(HEAD_DIM, dtype=jnp.int32) // 2)[None, :]
    place = jnp.where(
        pair < time,
        (positions // (GRID_H * GRID_W))[:, None],
        jnp.where(
            pair < time + side,
            (positions // GRID_W % GRID_H)[:, None],
            (positions % GRID_W)[:, None],
        ),
    ).astype(F32)
    angle = place * freq
    return jnp.cos(angle), jnp.sin(angle)


def prepare_kernel(q, qt, k, kt, v, vt, out, stats):
    for chip in range(CHIPS):
        for place, head in ((0, chip), (1, CHIPS + chip // 4)):
            columns = slice(head * HEAD_DIM, (head + 1) * HEAD_DIM)
            out[chip, place, :, :HEAD_DIM] = v[:, columns]
            out[chip, place, :, HEAD_DIM:] = vt[:, columns]
    lane = lax.broadcasted_iota(jnp.int32, (ROWS, HEAD_DIM), 1)
    total = jnp.zeros((ROWS, HEAD_DIM), F32)
    for place, (left, right) in enumerate(((q, q), (q, qt), (k, k), (k, kt))):
        product = left[...].astype(F32) * right[...].astype(F32)
        total = jnp.where(lane == place, jnp.sum(product, axis=1, keepdims=True), total)
    stats[...] = total


def prepare(*operands):
    return call(
        prepare_kernel,
        "prepare",
        [shape(CHIPS, 2, ROWS, 256), shape(ROWS, HEAD_DIM, kind=F32)],
        operands,
        [],
        60,
        cost(8 * ROWS * FEATURES, 6 * MIB),
    )


def norm_rope_kernel(q, qt, k, kt, mine, theirs, q_gain, k_gain, cosine, sine, out):
    stats = mine[...] + theirs[...]
    cos = cosine[...]
    even = lax.broadcasted_iota(jnp.int32, (ROWS, HEAD_DIM), 1) % 2 == 0
    sin_next = jnp.where(even, -sine[...], 0.0)
    sin_last = jnp.where(even, 0.0, sine[...])

    def rotated(x):
        after = pltpu.roll(x, HEAD_DIM - 1, 1)
        before = pltpu.roll(x, 1, 1)
        return (x * cos + (after * sin_next + before * sin_last)).astype(BF16)

    def of_head(raw_ref, tangent_ref, gain_ref, inverse, mixing, head):
        columns = slice(head * HEAD_DIM, (head + 1) * HEAD_DIM)
        raw = raw_ref[:, columns].astype(F32)
        tangent = tangent_ref[:, columns].astype(F32)
        gain = gain_ref[:, columns]
        normed = gain * raw * inverse
        normed_tangent = gain * (
            tangent * inverse - raw * mixing * inverse * inverse * inverse
        )
        return rotated(normed), rotated(normed_tangent)

    wide = (ROWS, HEAD_DIM)
    for first, raw_ref, tangent_ref, gain_ref in ((2, k, kt, k_gain), (0, q, qt, q_gain)):
        inverse = jnp.broadcast_to(lax.rsqrt(stats[:, first : first + 1] / HD + 1e-06), wide)
        mixing = jnp.broadcast_to(stats[:, first + 1 : first + 2] / HD, wide)
        for head in range(HEADS):
            turned = jnp.concatenate(
                of_head(raw_ref, tangent_ref, gain_ref, inverse, mixing, head), axis=1
            )
            low = 0 if first else 2 * ROWS
            if head < CHIPS:
                out[head, low : low + ROWS] = turned
                continue
            for column in range(4):
                chip = 4 * (head - CHIPS) + column
                if first:
                    out[chip, ROWS : 2 * ROWS] = turned
                else:
                    out[chip, 3 * ROWS :] = turned[column * PART : (column + 1) * PART]


def norm_rope(*operands):
    return call(
        norm_rope_kernel,
        "norm_rope",
        [shape(CHIPS, 2 * ROWS + SLOT, 256)],
        operands,
        [],
        60,
        cost(40 * ROWS * FEATURES, 5 * MIB),
    )[0]


def attend_kernel(mixed, mixed_other, v_in, v_other, out, keys, values, queries, results, sems):
    copies = []

    def copy(source, target):
        copies.append(pltpu.make_async_copy(source, target, sems.at[len(copies)]))
        copies[-1].start()

    main = CHIPS * ROWS
    for chip in range(CHIPS):
        copy(mixed.at[chip, 2 * ROWS : 3 * ROWS], queries.at[chip * ROWS : (chip + 1) * ROWS])
        low = main + chip * PART
        copy(mixed.at[chip, 3 * ROWS :], queries.at[low : low + PART])
    asked = len(copies)
    for place in range(2):
        for chunk in range(2 * CHIPS):
            rows = slice(chunk * ROWS, (chunk + 1) * ROWS)
            k_from, v_from = ((mixed, v_in), (mixed_other, v_other))[chunk // CHIPS]
            chip = chunk % CHIPS
            copy(k_from.at[chip, place * ROWS : (place + 1) * ROWS], keys.at[place, rows])
            copy(v_from.at[chip, place], values.at[place, rows])
    steps = 2 * CHIPS * ROWS // TILE_K
    group = 3 * TILE_K
    per_group = 2 * group // ROWS

    def one_tile(start, size, place, wait):
        both = queries[pl.ds(start, size)]
        plain = both[:, :HEAD_DIM]
        crossed = jnp.concatenate([both[:, HEAD_DIM:], plain], axis=1)
        weighted = jnp.zeros((size, 256), F32)
        weighted_tangent = jnp.zeros((size, HEAD_DIM), F32)
        norm_lanes = jnp.zeros((size, HEAD_DIM), F32)
        tangent_lanes = jnp.zeros((size, HEAD_DIM), F32)

        def rows(step):
            return slice(step * TILE_K, (step + 1) * TILE_K)

        def score(step):
            if wait and step % 3 == 0:
                low = asked + (place * steps + step) // 3 * per_group
                for member in copies[low : low + per_group]:
                    member.wait()
            key_rows = keys[place, rows(step)]
            return dot_rows(plain, key_rows[:, :HEAD_DIM]), dot_rows(crossed, key_rows)

        ahead, behind = score(0), None
        for step in range(steps + 1):
            if step < steps:
                scores, scores_tangent = ahead
                if step + 1 < steps:
                    ahead = score(step + 1)
                squashed = jnp.tanh(scores * (SCALE / CAP))
                weights = jnp.exp2(squashed * (CAP * math.log2(math.e)))
                weights_tangent = weights * (
                    (1.0 - squashed * squashed) * (scores_tangent * SCALE)
                )
                for low in range(0, TILE_K, HEAD_DIM):
                    norm_lanes = norm_lanes + weights[:, low : low + HEAD_DIM]
                    tangent_lanes = tangent_lanes + weights_tangent[:, low : low + HEAD_DIM]
            if step > 0:
                value_rows = values[place, rows(step - 1)]
                weighted = weighted + dot(behind[0], value_rows)
                weighted_tangent = weighted_tangent + dot(behind[1], value_rows[:, :HEAD_DIM])
            behind = (weights.astype(BF16), weights_tangent.astype(BF16))
        inverse = 1.0 / jnp.sum(norm_lanes, axis=1, keepdims=True)
        shift = jnp.sum(tangent_lanes, axis=1, keepdims=True) * inverse
        attention = weighted[:, :HEAD_DIM] * inverse
        attention_tangent = (
            weighted[:, HEAD_DIM:] + weighted_tangent
        ) * inverse - shift * attention
        outcome = jnp.concatenate([attention, attention_tangent], axis=1)
        results[pl.ds(start, size)] = outcome.astype(BF16)

    for member in copies[:asked]:
        member.wait()
    one_tile(0, TILE_Q, 0, True)

    def later(tile, carry):
        one_tile(pl.multiple_of(tile * TILE_Q, TILE_Q), TILE_Q, 0, False)
        return carry

    lax.fori_loop(1, main // TILE_Q, later, 0)
    one_tile(main, CHIPS * PART, 1, True)
    for group in range(2):
        for chip in range(CHIPS):
            out[group, chip, :ROWS] = results[chip * ROWS : (chip + 1) * ROWS]
            low = main + chip * PART
            out[group, chip, ROWS:] = results[low : low + PART]


def attend(*operands):
    anywhere = pl.BlockSpec(memory_space=pl.ANY)
    outs = [shape(2, CHIPS, SLOT, 256)]
    return pl.pallas_call(
        attend_kernel,
        grid=(1,),
        out_shape=outs,
        in_specs=[anywhere] * len(operands),
        out_specs=jax.tree.map(whole, outs),
        scratch_shapes=[
            pltpu.VMEM((2, 2 * CHIPS * ROWS, 256), BF16),
            pltpu.VMEM((2, 2 * CHIPS * ROWS, 256), BF16),
            pltpu.VMEM((CHIPS * SLOT, 256), BF16),
            pltpu.VMEM((CHIPS * SLOT, 256), BF16),
            pltpu.SemaphoreType.DMA((10 * CHIPS,)),
        ],
        compiler_params=params(60),
        cost_estimate=cost(8 * 256 * CHIPS * SLOT * 2 * CHIPS * ROWS, 14 * MIB),
        name="attend",
    )(*operands)[0]


def project_kernel(last, meta, parts, *refs):
    pieces, refs = refs[:4], refs[4:]
    before, refs = (refs[0], refs[1:]) if last else (None, refs)
    outs, left = refs[:-1], refs[-1]

    @pl.when(pl.program_id(0) == 0)
    def _():
        def column(head):
            return (head + HEADS - meta[1] * (HEADS // 2)) % HEADS

        for chip in range(CHIPS):
            part = parts.at[0, chip]
            for side in range(2):
                lanes = slice(side * HEAD_DIM, (side + 1) * HEAD_DIM)
                top = side * ROWS
                left[column(chip), top : top + ROWS] = part[:ROWS, lanes]
                low = top + chip % 4 * PART
                left[column(CHIPS + chip // 4), low : low + PART] = part[ROWS:, lanes]

    rows = jnp.concatenate([left[head] for head in range(HEADS)], axis=1)
    for low in range(0, FEATURES, 256):
        columns = slice(low, low + 256)
        right = jnp.concatenate([piece[0, :, columns] for piece in pieces], axis=0)
        result = dot(rows, right)
        if last:
            result = result + before[:, columns]
            outs[0][:, columns] = result[:ROWS].astype(BF16)
            outs[1][:, columns] = result[ROWS:].astype(BF16)
        else:
            outs[0][:, columns] = result


def project(meta, parts, weights, before=None):
    last = before is not None
    quarter = FEATURES // 4

    def straight(step, meta):
        return (2 * meta[2] + step, 0, 0)

    def mirrored(step, meta):
        return (3 - 2 * meta[2] - step, 0, 0)

    def of_group(step, meta):
        return (1 - meta[2] if last else meta[2], 0, 0, 0)

    def columns(rows):
        return pl.BlockSpec((rows, FEATURES), lambda step, meta: (0, step))

    specs = [pl.BlockSpec((1, CHIPS, SLOT, 256), of_group)]
    specs += [pl.BlockSpec((1, quarter, FEATURES), at) for at in (straight, mirrored)] * 2
    operands = [member for member in weights for _ in range(2)]
    if last:
        operands += [before]
        specs += [columns(2 * ROWS)]
        outs, out_specs = [shape(ROWS, 2 * FEATURES)] * 2, [columns(ROWS)] * 2
    else:
        outs, out_specs = [shape(2 * ROWS, 2 * FEATURES, kind=F32)], [columns(2 * ROWS)]
    return pl.pallas_call(
        functools.partial(project_kernel, last),
        out_shape=outs,
        grid_spec=pltpu.PrefetchScalarGridSpec(
            num_scalar_prefetch=1,
            grid=(2,),
            in_specs=specs,
            out_specs=out_specs,
            scratch_shapes=[pltpu.VMEM((HEADS, 2 * ROWS, HEAD_DIM), BF16)],
        ),
        compiler_params=params(60),
        cost_estimate=cost(2 * 2 * ROWS * FEATURES * 2 * FEATURES, 12 * MIB),
        name="project",
    )(meta, parts, *operands)


HOME = [(clip, group) for clip in range(4) for group in range(2) if clip // 2 == group]
AWAY = [(clip, group) for clip in range(4) for group in range(2) if clip // 2 != group]
CORES = [[2 * chip + core for chip in range(CHIPS)] for core in range(2)]
GROUP_CORES = [
    [16 * group + 2 * chip + core for group in range(2) for chip in range(CHIPS)]
    for core in range(2)
]


def to_chips(array):
    return lax.all_to_all(array, "ctx", 0, 0, axis_index_groups=CORES, tiled=True)


def to_core(array):
    return lax.ppermute(array, "ctx", [(place, place ^ 1) for place in range(16)])


def after(arrays, event):
    return lax.optimization_barrier((arrays, event))[0]


def move(array, pairs):
    links = []
    for (clip, group), (next_clip, next_group) in pairs:
        flip = 8 * (group ^ next_group)
        for place in range(16):
            source = 32 * clip + 16 * group + place
            links.append((source, 32 * next_clip + 16 * next_group + (place ^ flip)))
    return lax.ppermute(array, ("dp", "head", "ctx"), links)


def to_group(array):
    return lax.ppermute(array, "head", [(0, 1), (1, 0)])


def on_device(
    query_input,
    key_input,
    value_input,
    query_tangent,
    key_tangent,
    value_tangent,
    query_gain,
    key_gain,
    out_weight,
    span_order,
):
    place = lax.axis_index("ctx")
    group = lax.axis_index("head")
    chip, core = place // 2, place % 2
    meta = jnp.stack([chip, core, group]).astype(jnp.int32)
    raw = [
        member[0]
        for member in (
            query_input,
            query_tangent,
            key_input,
            key_tangent,
            value_input,
            value_tangent,
        )
    ]
    quarter = FEATURES // 4
    home = lax.axis_index("dp") // 2 == group
    lower, upper = [
        lax.dynamic_slice_in_dim(out_weight, (2 * core + part) * quarter, quarter, 0)
        for part in range(2)
    ]
    value_out, stats = prepare(*raw)
    second = move(after(upper, stats), [((clip, own), (3 - clip, own)) for clip, own in HOME])
    values = to_chips(value_out)
    stats_peer = to_group(stats)
    second, stats_peer, meta = lax.optimization_barrier((second, stats_peer, meta))
    cosine, sine = rope_tables(lax.dynamic_slice_in_dim(span_order, 2 * place, 2))
    gains = (query_gain[None], key_gain[None])
    values, stats_peer, cosine, sine, gains = lax.optimization_barrier(
        (values, stats_peer, cosine, sine, gains)
    )
    own_piece = jnp.where(home, lower, second)
    own_weight = lax.all_gather(own_piece, "dp", axis=0)
    values_other = to_core(values)
    near = move(after(lower, values), [((clip, own), (clip, 1 - own)) for clip, own in AWAY])
    far = move(after(upper, values), [((clip, own), (3 - clip, 1 - own)) for clip, own in AWAY])
    mixed_out = norm_rope(*raw[:4], stats, stats_peer, *gains, cosine, sine)
    mixed = to_chips(after(mixed_out, values_other))
    near, far = after((near, far), mixed)
    cross_weight = lax.all_gather(near + far, "dp", axis=0)
    mixed_other = to_core(mixed)
    own_other = to_core(after(own_weight, mixed_other))
    results = attend(mixed, mixed_other, values, values_other)
    parts = lax.all_to_all(
        results.reshape(2 * CHIPS, SLOT, 256),
        ("head", "ctx"),
        0,
        0,
        axis_index_groups=GROUP_CORES,
        tiled=True,
    )
    cross_other = to_core(after(cross_weight, parts))
    parts = parts.reshape(2, CHIPS, SLOT, 256)
    own = project(meta, parts, (own_weight, own_other))[0]
    projected, tangent = project(meta, parts, (cross_weight, cross_other), own)
    return (projected[None], tangent[None])


def solution(mesh):
    return jax.shard_map(
        on_device,
        mesh=mesh,
        in_specs=(
            P("dp", "ctx", "head"),
            P("dp", "ctx", "head"),
            P("dp", "ctx", "head"),
            P("dp", "ctx", "head"),
            P("dp", "ctx", "head"),
            P("dp", "ctx", "head"),
            P("head"),
            P("head"),
            P("head", "dp"),
            P(),
        ),
        out_specs=(P("dp", "ctx", "head"), P("dp", "ctx", "head")),
        check_vma=False,
    )
```

```python
import functools
import math

import jax
import jax.numpy as jnp
from jax import lax
from jax.experimental import pallas as pl
from jax.experimental.pallas import tpu as pltpu
from jax.sharding import PartitionSpec as P

HEAD_DIM = 128
GRID_H = 8
GRID_W = 16
CAP = 30
HD = 2560
SPAN = 96
ROWS = 192
HEADS = 10
FEATURES = HEADS * HEAD_DIM
CHIPS = 8
PART = 48
SLOT = ROWS + PART
TILE_Q = 384
TILE_K = 256
SCALE = 1.0 / math.sqrt(HEAD_DIM)
BF16 = jnp.bfloat16
F32 = jnp.float32
MIB = 2**20
SMEM = pl.BlockSpec(memory_space=pltpu.SMEM)


def params(mib):
    return pltpu.CompilerParams(vmem_limit_bytes=mib * MIB)


def cost(flops, moved):
    return pl.CostEstimate(flops=flops, bytes_accessed=moved, transcendentals=0)


def shape(*dims, kind=BF16):
    return jax.ShapeDtypeStruct(dims, kind)


def whole(member):
    return pl.BlockSpec(member.shape, lambda step: (0,) * len(member.shape))


def call(kernel, name, outs, operands, scratch, mib, estimate, scalars=0):
    return pl.pallas_call(
        kernel,
        grid=(1,),
        out_shape=outs,
        in_specs=[SMEM] * scalars + [whole(member) for member in operands[scalars:]],
        out_specs=jax.tree.map(whole, outs),
        scratch_shapes=scratch,
        compiler_params=params(mib),
        cost_estimate=estimate,
        name=name,
    )(*operands)


def dot(left, right):
    return lax.dot_general(left, right, (((1,), (0,)), ((), ())), preferred_element_type=F32)


def dot_rows(left, right):
    return lax.dot_general(left, right, (((1,), (1,)), ((), ())), preferred_element_type=F32)


def rope_tables(own_spans):
    positions = (
        own_spans[:, None] * SPAN + jnp.arange(SPAN, dtype=jnp.int32)[None, :]
    ).reshape(-1)
    pairs = HEAD_DIM // 2
    side = pairs // 3
    time = pairs - 2 * side
    time_freq = 10000.0 ** (-jnp.arange(time, dtype=F32) / time)
    side_freq = 10000.0 ** (-jnp.arange(side, dtype=F32) / side)
    freq = jnp.concatenate([time_freq, side_freq, side_freq])
    freq = jnp.broadcast_to(freq[:, None], (pairs, 2)).reshape(1, HEAD_DIM)
    pair = (jnp.arange(HEAD_DIM, dtype=jnp.int32) // 2)[None, :]
    place = jnp.where(
        pair < time,
        (positions // (GRID_H * GRID_W))[:, None],
        jnp.where(
            pair < time + side,
            (positions // GRID_W % GRID_H)[:, None],
            (positions % GRID_W)[:, None],
        ),
    ).astype(F32)
    angle = place * freq
    return jnp.cos(angle), jnp.sin(angle)


def prepare_kernel(q, qt, k, kt, v, vt, out, stats):
    for chip in range(CHIPS):
        for place, head in ((0, chip), (1, CHIPS + chip // 4)):
            columns = slice(head * HEAD_DIM, (head + 1) * HEAD_DIM)
            out[chip, place, :, :HEAD_DIM] = v[:, columns]
            out[chip, place, :, HEAD_DIM:] = vt[:, columns]
    lane = lax.broadcasted_iota(jnp.int32, (ROWS, HEAD_DIM), 1)
    total = jnp.zeros((ROWS, HEAD_DIM), F32)
    for place, (left, right) in enumerate(((q, q), (q, qt), (k, k), (k, kt))):
        product = left[...].astype(F32) * right[...].astype(F32)
        total = jnp.where(lane == place, jnp.sum(product, axis=1, keepdims=True), total)
    stats[...] = total


def prepare(*operands):
    return call(
        prepare_kernel,
        "prepare",
        [shape(CHIPS, 2, ROWS, 256), shape(ROWS, HEAD_DIM, kind=F32)],
        operands,
        [],
        60,
        cost(8 * ROWS * FEATURES, 6 * MIB),
    )


def norm_rope_kernel(q, qt, k, kt, mine, theirs, q_gain, k_gain, cosine, sine, out):
    stats = mine[...] + theirs[...]
    cos = cosine[...]
    even = lax.broadcasted_iota(jnp.int32, (ROWS, HEAD_DIM), 1) % 2 == 0
    sin_next = jnp.where(even, -sine[...], 0.0)
    sin_last = jnp.where(even, 0.0, sine[...])

    def rotated(x):
        after = pltpu.roll(x, HEAD_DIM - 1, 1)
        before = pltpu.roll(x, 1, 1)
        return (x * cos + (after * sin_next + before * sin_last)).astype(BF16)

    def of_head(raw_ref, tangent_ref, gain_ref, inverse, mixing, head):
        columns = slice(head * HEAD_DIM, (head + 1) * HEAD_DIM)
        raw = raw_ref[:, columns].astype(F32)
        tangent = tangent_ref[:, columns].astype(F32)
        gain = gain_ref[:, columns]
        normed = gain * raw * inverse
        normed_tangent = gain * (
            tangent * inverse - raw * mixing * inverse * inverse * inverse
        )
        return rotated(normed), rotated(normed_tangent)

    wide = (ROWS, HEAD_DIM)
    for first, raw_ref, tangent_ref, gain_ref in ((2, k, kt, k_gain), (0, q, qt, q_gain)):
        inverse = jnp.broadcast_to(lax.rsqrt(stats[:, first : first + 1] / HD + 1e-06), wide)
        mixing = jnp.broadcast_to(stats[:, first + 1 : first + 2] / HD, wide)
        for head in range(HEADS):
            turned = jnp.concatenate(
                of_head(raw_ref, tangent_ref, gain_ref, inverse, mixing, head), axis=1
            )
            low = 0 if first else 2 * ROWS
            if head < CHIPS:
                out[head, low : low + ROWS] = turned
                continue
            for column in range(4):
                chip = 4 * (head - CHIPS) + column
                if first:
                    out[chip, ROWS : 2 * ROWS] = turned
                else:
                    out[chip, 3 * ROWS :] = turned[column * PART : (column + 1) * PART]


def norm_rope(*operands):
    return call(
        norm_rope_kernel,
        "norm_rope",
        [shape(CHIPS, 2 * ROWS + SLOT, 256)],
        operands,
        [],
        60,
        cost(40 * ROWS * FEATURES, 5 * MIB),
    )[0]


def attend_kernel(mixed, mixed_other, v_in, v_other, out, keys, values, queries, results, sems):
    copies = []

    def copy(source, target):
        copies.append(pltpu.make_async_copy(source, target, sems.at[len(copies)]))
        copies[-1].start()

    main = CHIPS * ROWS
    for chip in range(CHIPS):
        copy(mixed.at[chip, 2 * ROWS : 3 * ROWS], queries.at[chip * ROWS : (chip + 1) * ROWS])
        low = main + chip * PART
        copy(mixed.at[chip, 3 * ROWS :], queries.at[low : low + PART])
    asked = len(copies)
    for place in range(2):
        for chunk in range(2 * CHIPS):
            rows = slice(chunk * ROWS, (chunk + 1) * ROWS)
            k_from, v_from = ((mixed, v_in), (mixed_other, v_other))[chunk // CHIPS]
            chip = chunk % CHIPS
            copy(k_from.at[chip, place * ROWS : (place + 1) * ROWS], keys.at[place, rows])
            copy(v_from.at[chip, place], values.at[place, rows])
    steps = 2 * CHIPS * ROWS // TILE_K
    group = 3 * TILE_K
    per_group = 2 * group // ROWS

    def one_tile(start, size, place, wait):
        both = queries[pl.ds(start, size)]
        plain = both[:, :HEAD_DIM]
        crossed = jnp.concatenate([both[:, HEAD_DIM:], plain], axis=1)
        weighted = jnp.zeros((size, 256), F32)
        weighted_tangent = jnp.zeros((size, HEAD_DIM), F32)
        norm_lanes = jnp.zeros((size, HEAD_DIM), F32)
        tangent_lanes = jnp.zeros((size, HEAD_DIM), F32)

        def rows(step):
            return slice(step * TILE_K, (step + 1) * TILE_K)

        def score(step):
            if wait and step % 3 == 0:
                low = asked + (place * steps + step) // 3 * per_group
                for member in copies[low : low + per_group]:
                    member.wait()
            key_rows = keys[place, rows(step)]
            return dot_rows(plain, key_rows[:, :HEAD_DIM]), dot_rows(crossed, key_rows)

        ahead, behind = score(0), None
        for step in range(steps + 1):
            if step < steps:
                scores, scores_tangent = ahead
                if step + 1 < steps:
                    ahead = score(step + 1)
                squashed = jnp.tanh(scores * (SCALE / CAP))
                weights = jnp.exp2(squashed * (CAP * math.log2(math.e)))
                weights_tangent = weights * (
                    (1.0 - squashed * squashed) * (scores_tangent * SCALE)
                )
                for low in range(0, TILE_K, HEAD_DIM):
                    norm_lanes = norm_lanes + weights[:, low : low + HEAD_DIM]
                    tangent_lanes = tangent_lanes + weights_tangent[:, low : low + HEAD_DIM]
            if step > 0:
                value_rows = values[place, rows(step - 1)]
                weighted = weighted + dot(behind[0], value_rows)
                weighted_tangent = weighted_tangent + dot(behind[1], value_rows[:, :HEAD_DIM])
            behind = (weights.astype(BF16), weights_tangent.astype(BF16))
        inverse = 1.0 / jnp.sum(norm_lanes, axis=1, keepdims=True)
        shift = jnp.sum(tangent_lanes, axis=1, keepdims=True) * inverse
        attention = weighted[:, :HEAD_DIM] * inverse
        attention_tangent = (
            weighted[:, HEAD_DIM:] + weighted_tangent
        ) * inverse - shift * attention
        outcome = jnp.concatenate([attention, attention_tangent], axis=1)
        results[pl.ds(start, size)] = outcome.astype(BF16)

    for member in copies[:asked]:
        member.wait()
    one_tile(0, TILE_Q, 0, True)

    def later(tile, carry):
        one_tile(pl.multiple_of(tile * TILE_Q, TILE_Q), TILE_Q, 0, False)
        return carry

    lax.fori_loop(1, main // TILE_Q, later, 0)
    one_tile(main, CHIPS * PART, 1, True)
    for group in range(2):
        for chip in range(CHIPS):
            out[group, chip, :ROWS] = results[chip * ROWS : (chip + 1) * ROWS]
            low = main + chip * PART
            out[group, chip, ROWS:] = results[low : low + PART]


def attend(*operands):
    anywhere = pl.BlockSpec(memory_space=pl.ANY)
    outs = [shape(2, CHIPS, SLOT, 256)]
    return pl.pallas_call(
        attend_kernel,
        grid=(1,),
        out_shape=outs,
        in_specs=[anywhere] * len(operands),
        out_specs=jax.tree.map(whole, outs),
        scratch_shapes=[
            pltpu.VMEM((2, 2 * CHIPS * ROWS, 256), BF16),
            pltpu.VMEM((2, 2 * CHIPS * ROWS, 256), BF16),
            pltpu.VMEM((CHIPS * SLOT, 256), BF16),
            pltpu.VMEM((CHIPS * SLOT, 256), BF16),
            pltpu.SemaphoreType.DMA((10 * CHIPS,)),
        ],
        compiler_params=params(60),
        cost_estimate=cost(8 * 256 * CHIPS * SLOT * 2 * CHIPS * ROWS, 14 * MIB),
        name="attend",
    )(*operands)[0]


def project_kernel(last, meta, parts, *refs):
    pieces, refs = refs[:4], refs[4:]
    before, refs = (refs[0], refs[1:]) if last else (None, refs)
    outs, left = refs[:-1], refs[-1]

    @pl.when(pl.program_id(0) == 0)
    def _():
        def column(head):
            return (head + HEADS - meta[1] * (HEADS // 2)) % HEADS

        for chip in range(CHIPS):
            part = parts.at[0, chip]
            for side in range(2):
                lanes = slice(side * HEAD_DIM, (side + 1) * HEAD_DIM)
                top = side * ROWS
                left[column(chip), top : top + ROWS] = part[:ROWS, lanes]
                low = top + chip % 4 * PART
                left[column(CHIPS + chip // 4), low : low + PART] = part[ROWS:, lanes]

    rows = jnp.concatenate([left[head] for head in range(HEADS)], axis=1)
    for low in range(0, FEATURES, 256):
        columns = slice(low, low + 256)
        right = jnp.concatenate([piece[0, :, columns] for piece in pieces], axis=0)
        result = dot(rows, right)
        if last:
            result = result + before[:, columns]
            outs[0][:, columns] = result[:ROWS].astype(BF16)
            outs[1][:, columns] = result[ROWS:].astype(BF16)
        else:
            outs[0][:, columns] = result


def project(meta, parts, weights, before=None):
    last = before is not None
    quarter = FEATURES // 4

    def straight(step, meta):
        return (2 * meta[2] + step, 0, 0)

    def mirrored(step, meta):
        return (3 - 2 * meta[2] - step, 0, 0)

    def of_group(step, meta):
        return (1 - meta[2] if last else meta[2], 0, 0, 0)

    def columns(rows):
        return pl.BlockSpec((rows, FEATURES), lambda step, meta: (0, step))

    specs = [pl.BlockSpec((1, CHIPS, SLOT, 256), of_group)]
    specs += [pl.BlockSpec((1, quarter, FEATURES), at) for at in (straight, mirrored)] * 2
    operands = [member for member in weights for _ in range(2)]
    if last:
        operands += [before]
        specs += [columns(2 * ROWS)]
        outs, out_specs = [shape(ROWS, 2 * FEATURES)] * 2, [columns(ROWS)] * 2
    else:
        outs, out_specs = [shape(2 * ROWS, 2 * FEATURES, kind=F32)], [columns(2 * ROWS)]
    return pl.pallas_call(
        functools.partial(project_kernel, last),
        out_shape=outs,
        grid_spec=pltpu.PrefetchScalarGridSpec(
            num_scalar_prefetch=1,
            grid=(2,),
            in_specs=specs,
            out_specs=out_specs,
            scratch_shapes=[pltpu.VMEM((HEADS, 2 * ROWS, HEAD_DIM), BF16)],
        ),
        compiler_params=params(63),
        cost_estimate=cost(2 * 2 * ROWS * FEATURES * 2 * FEATURES, 12 * MIB),
        name="project",
    )(meta, parts, *operands)


HOME = [(clip, group) for clip in range(4) for group in range(2) if clip // 2 == group]
AWAY = [(clip, group) for clip in range(4) for group in range(2) if clip // 2 != group]
CORES = [[2 * chip + core for chip in range(CHIPS)] for core in range(2)]
GROUP_CORES = [
    [16 * group + 2 * chip + core for group in range(2) for chip in range(CHIPS)]
    for core in range(2)
]


def to_chips(array):
    return lax.all_to_all(array, "ctx", 0, 0, axis_index_groups=CORES, tiled=True)


def to_core(array):
    return lax.ppermute(array, "ctx", [(place, place ^ 1) for place in range(16)])


def after(arrays, event):
    return lax.optimization_barrier((arrays, event))[0]


def move(array, pairs):
    links = []
    for (clip, group), (next_clip, next_group) in pairs:
        flip = 8 * (group ^ next_group)
        for place in range(16):
            source = 32 * clip + 16 * group + place
            links.append((source, 32 * next_clip + 16 * next_group + (place ^ flip)))
    return lax.ppermute(array, ("dp", "head", "ctx"), links)


def to_group(array):
    return lax.ppermute(array, "head", [(0, 1), (1, 0)])


def on_device(
    query_input,
    key_input,
    value_input,
    query_tangent,
    key_tangent,
    value_tangent,
    query_gain,
    key_gain,
    out_weight,
    span_order,
):
    place = lax.axis_index("ctx")
    group = lax.axis_index("head")
    chip, core = place // 2, place % 2
    meta = jnp.stack([chip, core, group]).astype(jnp.int32)
    raw = [
        member[0]
        for member in (
            query_input,
            query_tangent,
            key_input,
            key_tangent,
            value_input,
            value_tangent,
        )
    ]
    quarter = FEATURES // 4
    home = lax.axis_index("dp") // 2 == group
    lower, upper = [
        lax.dynamic_slice_in_dim(out_weight, (2 * core + part) * quarter, quarter, 0)
        for part in range(2)
    ]
    value_out, stats = prepare(*raw)
    second = move(after(upper, stats), [((clip, own), (3 - clip, own)) for clip, own in HOME])
    values = to_chips(value_out)
    stats_peer = to_group(stats)
    second, stats_peer, meta = lax.optimization_barrier((second, stats_peer, meta))
    cosine, sine = rope_tables(lax.dynamic_slice_in_dim(span_order, 2 * place, 2))
    gains = (query_gain[None], key_gain[None])
    values, stats_peer, cosine, sine, gains = lax.optimization_barrier(
        (values, stats_peer, cosine, sine, gains)
    )
    own_piece = jnp.where(home, lower, second)
    own_weight = lax.all_gather(own_piece, "dp", axis=0)
    values_other = to_core(values)
    near = move(after(lower, values), [((clip, own), (clip, 1 - own)) for clip, own in AWAY])
    far = move(after(upper, values), [((clip, own), (3 - clip, 1 - own)) for clip, own in AWAY])
    mixed_out = norm_rope(*raw[:4], stats, stats_peer, *gains, cosine, sine)
    mixed = to_chips(after(mixed_out, values_other))
    near, far = after((near, far), mixed)
    cross_weight = lax.all_gather(near + far, "dp", axis=0)
    mixed_other = to_core(mixed)
    own_other = to_core(after(own_weight, mixed_other))
    results = attend(mixed, mixed_other, values, values_other)
    parts = lax.all_to_all(
        results.reshape(2 * CHIPS, SLOT, 256),
        ("head", "ctx"),
        0,
        0,
        axis_index_groups=GROUP_CORES,
        tiled=True,
    )
    cross_other = to_core(after(cross_weight, parts))
    parts = parts.reshape(2, CHIPS, SLOT, 256)
    own = project(meta, parts, (own_weight, own_other))[0]
    projected, tangent = project(meta, parts, (cross_weight, cross_other), own)
    return (projected[None], tangent[None])


def solution(mesh):
    return jax.shard_map(
        on_device,
        mesh=mesh,
        in_specs=(
            P("dp", "ctx", "head"),
            P("dp", "ctx", "head"),
            P("dp", "ctx", "head"),
            P("dp", "ctx", "head"),
            P("dp", "ctx", "head"),
            P("dp", "ctx", "head"),
            P("head"),
            P("head"),
            P("head", "dp"),
            P(),
        ),
        out_specs=(P("dp", "ctx", "head"), P("dp", "ctx", "head")),
        check_vma=False,
    )
```
